32 devices in a mesh: wide: 8 (over z, x), narrow: 4 (over y, core).
Axes of the slice: x: 2, y: 2, z: 4, core: 2. Of those that a mesh axis runs over, the one named last changes fastest.
Arguments:
- totals: float32 [16, 256, 512], P('narrow', 'wide'), may hold values from 0.5 to 2
- courant: float32 [256, 512], P('wide'), may hold values from 0.05 to 0.4
- diffusion: float32 [256, 512], P('wide'), may hold values from 0.02 to 0.14
- stoich: float32 [32, 16], replicated, may hold values from 0 to 0.5
- log_k: float32 [32], replicated, may hold values from -2 to 0
- mineral_stoich: float32 [12, 16], replicated, may hold values from 0 to 0.5
- mineral_log_k: float32 [12], replicated, may hold values from 0 to 2
- mineral_rate: float32 [12], replicated, may hold values from 0.05 to 1
- front_counts: int32 [8, 4], replicated, may hold values from 0 to 16, as said below
- mineral_flags: int32 [128, 4], P('wide', 'narrow'), may hold values 0 or 1
Outputs:
- speciated: float32 [16, 256, 512], P(None, 'wide', 'narrow')
The draws below stay inside these ranges and needn't reach their ends.
Inputs may be any that keep to these rules, and one draw needn't show every extreme that they name: `front_counts`: some tile has all 16 of its blocks front.
All inputs are finite; a program needn't handle non-finite values. Where the reference program divides by a largest or mean magnitude, that divisor is 1e-20 or more. No bound on the sum of `mineral_flags` on one device may be relied on, other than what follows from the above.
Results may differ from the reference program's by a relative error of at most 0.0003.
Values sent between devices are 32-bit elements; how exact they have to be, the bound alone decides.
A program may use at most 64 MiB of HBM per device.

```python
import math
import jax
import jax.numpy as jnp
from jax import lax

NC = 16
NM = 12
NSEC = 32
CX = 32
YT = 128
STEPS = 4
ITERS = 4
NBLK = 16
NX = 256
NY = 512
N_NARROW = 4


def draw_front_counts(key, part):
    tiles_x = NX // CX
    tiles_y = NY // YT
    key_light, key_busy, key_full = jax.random.split(key, 3)
    light_load = jax.random.randint(key_light, (tiles_x, tiles_y), 0, NBLK // 4 + 1)
    busy_tile = jax.random.randint(key_busy, (tiles_x, tiles_y), 0, 8) == 0
    counts = jnp.where(busy_tile, NBLK, light_load).reshape(-1)
    chosen = jax.random.randint(key_full, (), 0, tiles_x * tiles_y)
    counts = counts.at[chosen].set(NBLK)
    return counts.reshape(tiles_x, tiles_y).astype(jnp.int32)


def place_ends(values, rng, low, high):
    place = [jax.random.randint(jax.random.fold_in(rng, axis), (), 0, length) for axis, length in enumerate(values.shape)]
    main_axis = values.shape.index(max(values.shape))
    next_to = place[:main_axis] + [(place[main_axis] + 1) % values.shape[main_axis]] + place[main_axis + 1:]
    return values.at[tuple(place)].set(low).at[tuple(next_to)].set(high)


def level_of(own_key, extent, cuts, least, high):
    def one(dim, blocks):
        draws = jax.random.uniform(jax.random.fold_in(jax.random.fold_in(own_key, 6), dim), (blocks,), jnp.float32, least / len(cuts), high / len(cuts))
        return jnp.repeat(jnp.exp(draws), extent[dim] // blocks).reshape((-1,) + (1,) * (len(extent) - dim - 1))

    level = one(*cuts[0])
    for cut in cuts[1:]:
        level = level * one(*cut)
    return level


def setup_inputs(seed: int = 0) -> dict:
    streams_of = jax.random.split(jax.random.key(seed), 11)
    totals = jnp.clip(0.5 + 1.5 * jax.random.uniform(streams_of[0], (NC, NX, NY), jnp.float32) ** level_of(streams_of[0], (NC, NX, NY), ((0, 4), (1, 8)), -0.2, 0.2), 0.5, 2.0)
    courant = jnp.clip(0.05 + 0.35 * jax.random.uniform(streams_of[1], (NX, NY), jnp.float32) ** level_of(streams_of[1], (NX, NY), ((0, 8),), -0.2, 0.2), 0.05, 0.4)
    diffusion = jnp.clip(0.02 + 0.12000000104308128 * jax.random.uniform(streams_of[2], (NX, NY), jnp.float32) ** level_of(streams_of[2], (NX, NY), ((0, 8),), -0.2, 0.2), 0.02, 0.14)
    stoich = jnp.clip(jax.random.uniform(streams_of[3], (NSEC, NC), jnp.float32, 0.0, 0.5), 0.0, 0.5)
    log_k = jnp.clip(jax.random.uniform(streams_of[4], (NSEC,), jnp.float32, -2.0, 0.0), -2.0, 0.0)
    mineral_stoich = jnp.clip(jax.random.uniform(streams_of[5], (NM, NC), jnp.float32, 0.0, 0.5), 0.0, 0.5)
    mineral_log_k = jnp.clip(jax.random.uniform(streams_of[6], (NM,), jnp.float32, 0.0, 2.0), 0.0, 2.0)
    mineral_rate = jnp.clip(jnp.exp(jax.random.uniform(streams_of[7], (NM,), jnp.float32, math.log(0.05), math.log(1.0))), 0.05, 1.0)
    front_counts = draw_front_counts(jax.random.fold_in(streams_of[10], 71), 0)
    mineral_flags = place_ends((jax.random.randint(streams_of[9], (NX // 2, N_NARROW), 0, 2) < 1).astype(jnp.int32), jax.random.fold_in(streams_of[9], 1), 0, 1)
    return {"totals": totals, "courant": courant, "diffusion": diffusion, "stoich": stoich, "log_k": log_k, "mineral_stoich": mineral_stoich, "mineral_log_k": mineral_log_k, "mineral_rate": mineral_rate, "front_counts": front_counts, "mineral_flags": mineral_flags}


def advance(fields, upwind, downwind, courant, diffusion):
    beside = jnp.pad(fields, ((0, 0), (0, 0), (1, 1)))
    return fields - courant * (fields - upwind) + diffusion * ((upwind + downwind) + (beside[:, :, :-2] + beside[:, :, 2:]) - 4.0 * fields)


def pair_table(matrix):
    return (matrix[:, :, None] * matrix[:, None, :]).reshape(matrix.shape[0], -1).T


def solve_batch(jacobian, residual):
    order = residual.shape[0]
    matrix_rows = [jacobian[i] for i in range(order)]
    values = [residual[i] for i in range(order)]
    for pivot_index in range(order):
        pivot_row = matrix_rows[pivot_index]
        for target in range(pivot_index + 1, order):
            factor = matrix_rows[target][pivot_index] / pivot_row[pivot_index]
            matrix_rows[target] = matrix_rows[target] - factor[None, :] * pivot_row
            values[target] = values[target] - factor * values[pivot_index]
    solution = [None] * order
    for pivot_index in reversed(range(order)):
        partial_sum = values[pivot_index]
        for column in range(pivot_index + 1, order):
            partial_sum = partial_sum - matrix_rows[pivot_index][column] * solution[column]
        solution[pivot_index] = partial_sum / matrix_rows[pivot_index][pivot_index]
    return jnp.stack(solution)


def speciate(total, mineral_on, stoich, log_k, mineral_stoich, mineral_log_k, mineral_rate, pair_sec, pair_min):
    highest = lax.Precision.HIGHEST
    order = total.shape[0]
    free_log = jnp.log(total)
    for repeat in range(ITERS):
        free_conc = jnp.exp(free_log)
        secondary = jnp.exp(log_k[:, None] + jnp.dot(stoich, free_log, precision=highest))
        saturation = mineral_rate[:, None] * jnp.exp(jnp.dot(mineral_stoich, free_log, precision=highest) - mineral_log_k[:, None])
        residual = free_conc + jnp.dot(stoich.T, secondary, precision=highest) + mineral_on * jnp.dot(mineral_stoich.T, saturation, precision=highest) - total
        jacobian = jnp.dot(pair_sec, secondary, precision=highest) + mineral_on * jnp.dot(pair_min, saturation, precision=highest)
        jacobian = jacobian.reshape(order, order, -1) + jnp.eye(order, dtype=jnp.float32)[:, :, None] * free_conc[:, None, :]
        newton_step = solve_batch(jacobian, residual)
        largest = jnp.max(jnp.abs(newton_step), axis=0)
        free_log = free_log - newton_step / jnp.maximum(largest, 1.0)
    return free_log


def reference(totals, courant, diffusion, stoich, log_k, mineral_stoich, mineral_log_k, mineral_rate, front_counts, mineral_flags):
    fields = totals
    for repeat in range(STEPS):
        padded = jnp.pad(fields, ((0, 0), (1, 1), (0, 0)))
        fields = advance(fields, padded[:, :-2], padded[:, 2:], courant, diffusion)
    pair_sec = pair_table(stoich)
    pair_min = pair_table(mineral_stoich)
    tiles_y = NY // YT

    def one_pair(row_pair):
        rows_here = lax.dynamic_slice_in_dim(fields, row_pair * 2, 2, 1)
        blocks = rows_here.reshape(NC, 2, tiles_y, YT).transpose(2, 0, 1, 3).reshape(tiles_y, NC, 2 * YT)
        flag_row = mineral_flags[row_pair].astype(jnp.float32)
        solved = jax.vmap(lambda block, mineral_on: speciate(block, mineral_on, stoich, log_k, mineral_stoich, mineral_log_k, mineral_rate, pair_sec, pair_min))(blocks, flag_row)
        is_front = (row_pair % NBLK) < front_counts[row_pair // NBLK]
        chosen = jnp.where(is_front[:, None, None], solved, jnp.log(blocks))
        return chosen.reshape(tiles_y, NC, 2, YT).transpose(1, 2, 0, 3).reshape(NC, 2, NY)

    speciated = lax.map(one_pair, jnp.arange(NX // 2, dtype=jnp.int32))
    return speciated.transpose(1, 0, 2, 3).reshape(NC, NX, NY)
```

```python
import functools

import jax
import jax.numpy as jnp
from jax import lax
from jax.experimental import pallas as pl
from jax.experimental.pallas import tpu as pltpu
from jax.sharding import PartitionSpec as P

STEPS = 4
ITERS = 4
MESH = pl.DeviceIdType.MESH


def transport_kernel(
    wide_count,
    narrow_count,
    totals_ref,
    courant_ref,
    diffusion_ref,
    out_ref,
    halo_f,
    halo_c,
    halo_d,
    staged,
    halo_send,
    halo_recv,
    swap_send,
    swap_recv,
):
    components, rows, columns = totals_ref.shape
    halo = halo_c.shape[1]
    width = out_ref.shape[2]
    wide = lax.axis_index("wide")
    narrow = lax.axis_index("narrow")
    has_above = wide > 0
    has_below = wide < wide_count - 1
    peers = [lax.rem(narrow + d, narrow_count) for d in range(1, narrow_count)]

    barrier = pltpu.get_barrier_semaphore()
    for peer in peers:
        pl.semaphore_signal(barrier, inc=1, device_id=(wide, peer), device_id_type=MESH)

    @pl.when(has_above)
    def _():
        pl.semaphore_signal(barrier, inc=1, device_id=(wide - 1, narrow), device_id_type=MESH)

    @pl.when(has_below)
    def _():
        pl.semaphore_signal(barrier, inc=1, device_id=(wide + 1, narrow), device_id_type=MESH)

    neighbours = narrow_count - 1 + has_above.astype(jnp.int32) + has_below.astype(jnp.int32)
    pl.semaphore_wait(barrier, neighbours)

    low, high = pl.ds(0, halo), pl.ds(rows - halo, halo)

    def halo_copies(side, target, part):
        pairs = (
            (totals_ref.at[:, part, :], halo_f.at[side]),
            (courant_ref.at[part, :], halo_c.at[side]),
            (diffusion_ref.at[part, :], halo_d.at[side]),
        )
        return [
            pltpu.make_async_remote_copy(
                src_ref=src,
                dst_ref=dst,
                send_sem=halo_send.at[side, k],
                recv_sem=halo_recv.at[side, k],
                device_id=(target, narrow),
                device_id_type=MESH,
            )
            for k, (src, dst) in enumerate(pairs)
        ]

    to_below = halo_copies(0, wide + 1, high)
    to_above = halo_copies(1, wide - 1, low)

    @pl.when(has_below)
    def _():
        for copy in to_below:
            copy.start()

    @pl.when(has_above)
    def _():
        for copy in to_above:
            copy.start()

    def clear(side):
        halo_f[side] = jnp.zeros_like(halo_f[side])
        halo_c[side] = jnp.zeros_like(halo_c[side])
        halo_d[side] = jnp.zeros_like(halo_d[side])

    @pl.when(jnp.logical_not(has_above))
    def _():
        clear(0)

    @pl.when(jnp.logical_not(has_below))
    def _():
        clear(1)

    @pl.when(has_above)
    def _():
        for copy in to_below:
            copy.wait_recv()

    @pl.when(has_below)
    def _():
        for copy in to_above:
            copy.wait_recv()

    courant = jnp.concatenate([halo_c[0], courant_ref[...], halo_c[1]], axis=0)
    diffusion = jnp.concatenate([halo_d[0], diffusion_ref[...], halo_d[1]], axis=0)
    column = lax.broadcasted_iota(jnp.int32, courant.shape, 1)
    first, last = column == 0, column == columns - 1
    tall = rows + 2 * halo
    swaps = []
    for c in range(components):
        fields = jnp.concatenate([halo_f[0, c], totals_ref[c], halo_f[1, c]], axis=0)
        for _ in range(STEPS):
            upwind = pltpu.roll(fields, 1, 0)
            downwind = pltpu.roll(fields, tall - 1, 0)
            left = jnp.where(first, 0.0, pltpu.roll(fields, 1, 1))
            right = jnp.where(last, 0.0, pltpu.roll(fields, columns - 1, 1))
            fields = (
                fields
                - courant * (fields - upwind)
                + diffusion * ((upwind + downwind) + (left + right) - 4.0 * fields)
            )
        for p in range(narrow_count):
            staged[p, c] = fields[halo : halo + rows, p * width : (p + 1) * width]
        for k, peer in enumerate(peers):
            copy = pltpu.make_async_remote_copy(
                src_ref=staged.at[peer, c],
                dst_ref=out_ref.at[narrow * components + c],
                send_sem=swap_send.at[c, k],
                recv_sem=swap_recv.at[c, k],
                device_id=(wide, peer),
                device_id_type=MESH,
            )
            copy.start()
            swaps.append(copy)
        out_ref[narrow * components + c] = staged[narrow, c]

    @pl.when(has_below)
    def _():
        for copy in to_below:
            copy.wait_send()

    @pl.when(has_above)
    def _():
        for copy in to_above:
            copy.wait_send()

    for copy in swaps:
        copy.wait()


def transport(totals, courant, diffusion):
    components, rows, columns = totals.shape
    wide_count, narrow_count = lax.axis_size("wide"), lax.axis_size("narrow")
    halo = 8
    width = columns // narrow_count
    vmem = pl.BlockSpec(memory_space=pltpu.VMEM)
    return pl.pallas_call(
        functools.partial(transport_kernel, wide_count, narrow_count),
        out_shape=jax.ShapeDtypeStruct((components * narrow_count, rows, width), jnp.float32),
        in_specs=[vmem] * 3,
        out_specs=vmem,
        scratch_shapes=[
            pltpu.VMEM((2, components, halo, columns), jnp.float32),
            pltpu.VMEM((2, halo, columns), jnp.float32),
            pltpu.VMEM((2, halo, columns), jnp.float32),
            pltpu.VMEM((narrow_count, components, rows, width), jnp.float32),
            pltpu.SemaphoreType.DMA((2, 3)),
            pltpu.SemaphoreType.DMA((2, 3)),
            pltpu.SemaphoreType.DMA((components, narrow_count - 1)),
            pltpu.SemaphoreType.DMA((components, narrow_count - 1)),
        ],
        compiler_params=pltpu.CompilerParams(
            collective_id=0, has_side_effects=True, vmem_limit_bytes=24 * 2**20
        ),
        name="transport",
    )(totals, courant, diffusion)


def parts(values, count):
    found = []
    for _ in range(count):
        part = values.astype(jnp.bfloat16)
        found.append(part)
        values = values - part.astype(jnp.float32)
    return found


def solve_spd(entry, right):
    order = len(right)
    lower, scaled, inverse = {}, {}, []
    start = 0
    while start < order:
        size = 2 if start < order // 2 else order - start
        block = range(start, start + size)
        work = {}
        for j in block:
            for i in range(j, order + 1):
                work[i, j] = right[j] if i == order else entry(i, j)
        for k in range(start):
            for i in range(start, order + 1):
                for j in block:
                    if i >= j:
                        work[i, j] = work[i, j] - lower[i, k] * scaled[j, k]
        for k in block:
            inverse.append(1.0 / work[k, k])
            for i in range(k + 1, order + 1):
                scaled[i, k] = work[i, k]
                lower[i, k] = work[i, k] * inverse[k]
            for j in range(k + 1, start + size):
                for i in range(j, order + 1):
                    work[i, j] = work[i, j] - lower[i, k] * scaled[j, k]
        start += size
    found = [lower[order, j] for j in range(order)]
    for i in reversed(range(order)):
        for j in range(i):
            found[j] = found[j] - lower[i, j] * found[i]
    return found


def newton_kernel(
    secondary_count,
    counts_ref,
    flags_ref,
    totals_ref,
    wide_table_ref,
    tall_table_ref,
    offset_ref,
    out_ref,
    exponent_lhs,
    pair_f32,
    pair_lhs,
    y_ref,
    sums_ref,
):
    order, group, width = totals_ref.shape
    species = wide_table_ref.shape[0]
    pairs = order * (order + 1) // 2
    step = pl.program_id(0)
    place = {}
    for i in range(order):
        for j in range(i, order):
            place[j, i] = len(place)

    @pl.when(step == 0)
    def _():
        first, second, third = parts(wide_table_ref[...], 3)
        lane = lax.broadcasted_iota(jnp.int32, wide_table_ref.shape, 1) // order
        use_second = jnp.logical_or(lane == 2, lane == 5)
        table = jnp.where(
            use_second,
            second.astype(jnp.float32),
            jnp.where(lane == 4, third.astype(jnp.float32), first.astype(jnp.float32)),
        )
        exponent_lhs[...] = table.astype(jnp.bfloat16)
        pair_f32[...] = jnp.zeros_like(pair_f32)
        tall = tall_table_ref[...]
        for i in range(order):
            start = place[i, i]
            pair_f32[start : start + order - i, :] = tall[i:order, :] * tall[i : i + 1, :]
        pair_f32[pairs : pairs + order, :] = tall
        table = pair_f32[...]
        first, second = parts(table, 2)
        lane = lax.broadcasted_iota(jnp.int32, table.shape, 1)
        table = jnp.where(
            lane < 2 * species, first.astype(jnp.float32), second.astype(jnp.float32)
        )
        pair_lhs[...] = table.astype(jnp.bfloat16)

    for i in range(order):
        y_ref[i * group : (i + 1) * group, :] = jnp.log(totals_ref[i])

    count = counts_ref[lax.axis_index("wide"), lax.axis_index("narrow")]

    @pl.when(step * group < 2 * count)
    def _():
        offset = offset_ref[...]
        offset = jnp.concatenate([offset, offset], axis=1)
        lane = lax.broadcasted_iota(jnp.int32, (1, 2 * width), 1)

        def iterate(_, carry):
            for s in range(0, group, 2):
                y = jnp.concatenate(
                    [y_ref[pl.ds(s + h, order, stride=group), :] for h in range(2)], axis=1
                )
                y1, y2, y3 = parts(y, 3)
                exponent = jnp.dot(
                    exponent_lhs[...],
                    jnp.concatenate([y1, y2, y1, y3, y1, y2], axis=0),
                    preferred_element_type=jnp.float32,
                )
                x = jnp.exp(exponent + offset)
                flags = [
                    flags_ref[(step * group + s + h) // 2, 0].astype(jnp.float32) for h in range(2)
                ]
                on = jnp.where(lane < width, flags[0], flags[1])
                x = jnp.concatenate([x[:secondary_count], x[secondary_count:] * on], axis=0)
                x1, x2 = parts(x, 2)
                sums = jnp.dot(
                    pair_lhs[...],
                    jnp.concatenate([x1, x2, x1, x2], axis=0),
                    preferred_element_type=jnp.float32,
                )
                for h in range(2):
                    sums_ref[pl.ds(s + h, pairs + order, stride=group), :] = sums[
                        : pairs + order, h * width : (h + 1) * width
                    ]

            def total(p):
                return sums_ref[p * group : (p + 1) * group, :]

            old = [y_ref[i * group : (i + 1) * group, :] for i in range(order)]
            free = [jnp.exp(v) for v in old]
            residual = [free[i] + total(pairs + i) - totals_ref[i] for i in range(order)]

            def entry(i, j):
                value = total(place[i, j])
                return value + free[i] if i == j else value

            delta = solve_spd(entry, residual)
            largest = [jnp.abs(v) for v in delta]
            while len(largest) > 1:
                largest = [
                    jnp.maximum(a, b) for a, b in zip(largest[::2], largest[1::2])
                ] + largest[len(largest) // 2 * 2 :]
            scale = 1.0 / jnp.maximum(largest[0], 1.0)
            for i in range(order):
                y_ref[i * group : (i + 1) * group, :] = y_ref[
                    i * group : (i + 1) * group, :
                ] - delta[i] * scale
            return carry

        lax.fori_loop(0, ITERS, iterate, 0)

    row = step * group + lax.broadcasted_iota(jnp.int32, (group, width), 0)
    front = row < 2 * count
    for i in range(order):
        out_ref[i] = jnp.where(
            front, y_ref[i * group : (i + 1) * group, :], jnp.log(totals_ref[i])
        )


def speciate(
    totals, stoich, log_k, mineral_stoich, mineral_log_k, mineral_rate, front_counts, flags
):
    order, rows, width = totals.shape
    group = 8
    secondary_count, mineral_count = stoich.shape[0], mineral_stoich.shape[0]
    used = secondary_count + mineral_count
    species = -(-used // 16) * 16
    table = jnp.pad(jnp.concatenate([stoich, mineral_stoich], axis=0), ((0, species - used), (0, 0)))
    offset = jnp.pad(
        jnp.concatenate([log_k, jnp.log(mineral_rate) - mineral_log_k]), (0, species - used)
    )
    offset = jnp.broadcast_to(offset[:, None], (species, width))
    wide_table = jnp.tile(table, (1, 6))
    tall_table = jnp.tile(table.T, (1, 4))
    sums = order * (order + 1) // 2 + order
    sums_padded = -(-sums // 16) * 16
    smem = pl.BlockSpec(memory_space=pltpu.SMEM)
    whole = pl.BlockSpec(memory_space=pltpu.VMEM)
    block = pl.BlockSpec((order, group, width), lambda i: (0, i, 0))
    return pl.pallas_call(
        functools.partial(newton_kernel, secondary_count),
        grid=(rows // group,),
        out_shape=jax.ShapeDtypeStruct(totals.shape, jnp.float32),
        in_specs=[smem, smem, block, whole, whole, whole],
        out_specs=block,
        scratch_shapes=[
            pltpu.VMEM((species, 6 * order), jnp.bfloat16),
            pltpu.VMEM((sums_padded, 4 * species), jnp.float32),
            pltpu.VMEM((sums_padded, 4 * species), jnp.bfloat16),
            pltpu.VMEM((order * group, width), jnp.float32),
            pltpu.VMEM((sums * group, width), jnp.float32),
        ],
        compiler_params=pltpu.CompilerParams(vmem_limit_bytes=24 * 2**20),
        name="newton",
    )(front_counts, flags, totals, wide_table, tall_table, offset)


def shards(
    totals,
    courant,
    diffusion,
    stoich,
    log_k,
    mineral_stoich,
    mineral_log_k,
    mineral_rate,
    front_counts,
    mineral_flags,
):
    moved = transport(totals, courant, diffusion)
    return speciate(
        moved,
        stoich,
        log_k,
        mineral_stoich,
        mineral_log_k,
        mineral_rate,
        front_counts,
        mineral_flags,
    )


def solution(mesh):
    placed = (
        P("narrow", "wide", None),
        P("wide", None),
        P("wide", None),
        P(),
        P(),
        P(),
        P(),
        P(),
        P(),
        P("wide", "narrow"),
    )
    return jax.shard_map(
        shards, mesh=mesh, in_specs=placed, out_specs=P(None, "wide", "narrow"), check_vma=False
    )
```

```python
import functools

import jax
import jax.numpy as jnp
from jax import lax
from jax.experimental import pallas as pl
from jax.experimental.pallas import tpu as pltpu
from jax.sharding import PartitionSpec as P

STEPS = 4
ITERS = 4
MESH = pl.DeviceIdType.MESH


def parts(values, count):
    found = []
    for _ in range(count):
        part = values.astype(jnp.bfloat16)
        found.append(part)
        values = values - part.astype(jnp.float32)
    return found


def column_of(row):
    count = row.shape[1]
    shape = (count, count)
    same = lax.broadcasted_iota(jnp.int32, shape, 0) == lax.broadcasted_iota(jnp.int32, shape, 1)
    return jnp.sum(jnp.where(same, jnp.broadcast_to(row, shape), 0.0), axis=1, keepdims=True)


def build_tables(stoich, log_k, mineral_stoich, mineral_log_k, mineral_rate, refs):
    exponent_out, pair_out, offset_out, wide_f32, pair_f32 = refs
    order = stoich.shape[0]
    species, width = offset_out.shape
    split, used = stoich.shape[1], stoich.shape[1] + mineral_stoich.shape[0]
    offset_out[...] = jnp.zeros_like(offset_out)
    offset_out[0:split, :] = jnp.broadcast_to(column_of(log_k[...]), (split, width))
    offset_out[split:used, :] = jnp.broadcast_to(
        column_of(jnp.log(mineral_rate[...]) - mineral_log_k[...]), (used - split, width)
    )

    def copies(length, first, period, lanes):
        row = lax.broadcasted_iota(jnp.int32, (length, lanes), 0) + first
        lane = lax.broadcasted_iota(jnp.int32, (length, lanes), 1)
        return jnp.where(lane % period == row, 1.0, 0.0).astype(jnp.float32)

    def product(left, right, dim):
        return lax.dot_general(
            left,
            right,
            (((dim,), (0,)), ((), ())),
            precision=lax.Precision.HIGHEST,
            preferred_element_type=jnp.float32,
        )

    spread = copies(order, 0, order, 6 * order)
    wide_f32[...] = jnp.zeros_like(wide_f32)
    wide_f32[0:split, :] = product(stoich[...], spread, 0)
    wide_f32[split:used, :] = product(mineral_stoich[...], spread, 1)
    wide = wide_f32[...]
    first, second, third = parts(wide, 3)
    lane = lax.broadcasted_iota(jnp.int32, wide.shape, 1) // order
    exponent_out[...] = jnp.where(
        jnp.logical_or(lane == 2, lane == 5),
        second.astype(jnp.float32),
        jnp.where(lane == 4, third.astype(jnp.float32), first.astype(jnp.float32)),
    ).astype(jnp.bfloat16)
    tall = product(stoich[...], copies(split, 0, species, 4 * species), 1) + product(
        mineral_stoich[...], copies(used - split, split, species, 4 * species), 0
    )
    pair_f32[...] = jnp.zeros_like(pair_f32)
    start = 0
    for i in range(order):
        pair_f32[start : start + order - i, :] = tall[i:order, :] * tall[i : i + 1, :]
        start += order - i
    pair_f32[start : start + order, :] = tall
    first, second = parts(pair_f32[...], 2)
    lane = lax.broadcasted_iota(jnp.int32, pair_f32.shape, 1)
    pair_out[...] = jnp.where(
        lane < 2 * species, first.astype(jnp.float32), second.astype(jnp.float32)
    ).astype(jnp.bfloat16)


def transport_kernel(
    wide_count,
    narrow_count,
    totals_any,
    courant_any,
    diffusion_any,
    stoich_any,
    log_k_any,
    mineral_stoich_any,
    mineral_log_k_any,
    mineral_rate_any,
    counts_any,
    flags_any,
    out_ref,
    exponent_out,
    pair_out,
    offset_out,
    on_out,
    front_out,
    tall_f,
    tall_c,
    tall_d,
    stoich,
    log_k,
    mineral_stoich,
    mineral_log_k,
    mineral_rate,
    counts,
    flags,
    halo_out,
    halo_in,
    staged,
    wide_f32,
    pair_f32,
    local_sem,
    halo_send,
    halo_recv,
    swap_send,
    swap_recv,
):
    components, tall, columns = tall_f.shape
    rows, width = out_ref.shape[1:]
    pad = (tall - rows) // 2
    wide = lax.axis_index("wide")
    narrow = lax.axis_index("narrow")
    has_above = wide > 0
    has_below = wide < wide_count - 1
    peers = [lax.rem(narrow + d, narrow_count) for d in range(1, narrow_count)]
    inside = pl.ds(pad, rows)

    moves = [
        pltpu.make_async_copy(src, dst, local_sem.at[k])
        for k, (src, dst) in enumerate(
            (
                (totals_any, tall_f.at[:, inside, :]),
                (courant_any, tall_c.at[inside, :]),
                (diffusion_any, tall_d.at[inside, :]),
                (stoich_any, stoich),
                (log_k_any, log_k),
                (mineral_stoich_any, mineral_stoich),
                (mineral_log_k_any, mineral_log_k),
                (mineral_rate_any, mineral_rate),
                (counts_any, counts),
                (flags_any, flags),
            )
        )
    ]
    for move in moves:
        move.start()

    barrier = pltpu.get_barrier_semaphore()
    for peer in peers:
        pl.semaphore_signal(barrier, inc=1, device_id=(wide, peer), device_id_type=MESH)

    @pl.when(has_above)
    def _():
        pl.semaphore_signal(barrier, inc=1, device_id=(wide - 1, narrow), device_id_type=MESH)

    @pl.when(has_below)
    def _():
        pl.semaphore_signal(barrier, inc=1, device_id=(wide + 1, narrow), device_id_type=MESH)

    for ref in (tall_c, tall_d):
        for start in (0, pad + rows):
            ref[start : start + pad, :] = jnp.zeros((pad, columns), jnp.float32)
    for start in (0, pad + rows):
        tall_f[:, start : start + pad, :] = jnp.zeros((components, pad, columns), jnp.float32)

    for move in moves[:3]:
        move.wait()

    for side, start in ((0, pad + rows - STEPS), (1, pad)):
        for c in range(components):
            halo_out[side, c * STEPS : (c + 1) * STEPS, :] = tall_f[c, start : start + STEPS, :]
        end = components * STEPS
        halo_out[side, end : end + STEPS, :] = tall_c[start : start + STEPS, :]
        halo_out[side, end + STEPS : end + 2 * STEPS, :] = tall_d[start : start + STEPS, :]

    neighbours = narrow_count - 1 + has_above.astype(jnp.int32) + has_below.astype(jnp.int32)
    pl.semaphore_wait(barrier, neighbours)

    def halo_copy(side, target):
        return pltpu.make_async_remote_copy(
            src_ref=halo_out.at[side],
            dst_ref=halo_in.at[side],
            send_sem=halo_send.at[side],
            recv_sem=halo_recv.at[side],
            device_id=(target, narrow),
            device_id_type=MESH,
        )

    to_below = halo_copy(0, wide + 1)
    to_above = halo_copy(1, wide - 1)

    @pl.when(has_below)
    def _():
        to_below.start()

    @pl.when(has_above)
    def _():
        to_above.start()

    for move in moves[3:]:
        move.wait()
    build_tables(
        stoich,
        log_k,
        mineral_stoich,
        mineral_log_k,
        mineral_rate,
        (exponent_out, pair_out, offset_out, wide_f32, pair_f32),
    )
    blocks = flags.shape[1]
    row = lax.broadcasted_iota(jnp.int32, (rows, blocks), 0)
    mine = row // (rows // blocks) == lax.broadcasted_iota(jnp.int32, (rows, blocks), 1)
    flag_rows = jnp.broadcast_to(flags[...].astype(jnp.float32), (rows, blocks))
    on = jnp.sum(jnp.where(mine, flag_rows, 0.0), axis=1, keepdims=True)
    on_out[...] = jnp.broadcast_to(on, on_out.shape)
    row = lax.broadcasted_iota(jnp.int32, counts.shape, 0)
    lane = lax.broadcasted_iota(jnp.int32, counts.shape, 1)
    own = jnp.where(
        jnp.logical_and(row == narrow, lane == wide), counts[...].astype(jnp.float32), 0.0
    )
    own = jnp.sum(jnp.sum(own, axis=1, keepdims=True), axis=0, keepdims=True)
    row = lax.broadcasted_iota(jnp.int32, front_out.shape, 0) // (rows // blocks)
    front_out[...] = jnp.where(row.astype(jnp.float32) < own, 1.0, 0.0)

    def take(side, start):
        for c in range(components):
            tall_f[c, start : start + STEPS, :] = halo_in[side, c * STEPS : (c + 1) * STEPS, :]
        end = components * STEPS
        tall_c[start : start + STEPS, :] = halo_in[side, end : end + STEPS, :]
        tall_d[start : start + STEPS, :] = halo_in[side, end + STEPS : end + 2 * STEPS, :]

    @pl.when(has_above)
    def _():
        to_below.wait_recv()
        take(0, pad - STEPS)

    @pl.when(has_below)
    def _():
        to_above.wait_recv()
        take(1, pad + rows)

    courant = tall_c[...]
    diffusion = tall_d[...]
    column = lax.broadcasted_iota(jnp.int32, courant.shape, 1)
    first, last = column == 0, column == columns - 1
    swaps = []
    for c in range(components):
        fields = tall_f[c]
        for _ in range(STEPS):
            upwind = pltpu.roll(fields, 1, 0)
            downwind = pltpu.roll(fields, tall - 1, 0)
            left = jnp.where(first, 0.0, pltpu.roll(fields, 1, 1))
            right = jnp.where(last, 0.0, pltpu.roll(fields, columns - 1, 1))
            fields = (
                fields
                - courant * (fields - upwind)
                + diffusion * ((upwind + downwind) + (left + right) - 4.0 * fields)
            )
        for p in range(narrow_count):
            staged[p, c] = fields[pad : pad + rows, p * width : (p + 1) * width]
        for k, peer in enumerate(peers):
            copy = pltpu.make_async_remote_copy(
                src_ref=staged.at[peer, c],
                dst_ref=out_ref.at[narrow * components + c],
                send_sem=swap_send.at[c, k],
                recv_sem=swap_recv.at[c, k],
                device_id=(wide, peer),
                device_id_type=MESH,
            )
            copy.start()
            swaps.append(copy)
        out_ref[narrow * components + c] = staged[narrow, c]

    @pl.when(has_below)
    def _():
        to_below.wait_send()

    @pl.when(has_above)
    def _():
        to_above.wait_send()

    for copy in swaps:
        copy.wait()


def transport(
    totals,
    courant,
    diffusion,
    stoich,
    log_k,
    mineral_stoich,
    mineral_log_k,
    mineral_rate,
    front_counts,
    mineral_flags,
):
    components, rows, columns = totals.shape
    wide_count, narrow_count = lax.axis_size("wide"), lax.axis_size("narrow")
    width = columns // narrow_count
    order = components * narrow_count
    tall = rows + 2 * 8
    packed = (components + 2) * STEPS
    species = -(-(stoich.shape[0] + mineral_stoich.shape[0]) // 16) * 16
    sums = order * (order + 1) // 2 + order
    sums_padded = -(-sums // 16) * 16
    vmem = pl.BlockSpec(memory_space=pltpu.VMEM)
    small = (
        stoich.T,
        log_k.reshape(1, -1),
        mineral_stoich,
        mineral_log_k.reshape(1, -1),
        mineral_rate.reshape(1, -1),
        front_counts.T,
        mineral_flags.reshape(1, -1),
    )
    f32 = jnp.float32
    outs = (
        ((order, rows, width), f32),
        ((species, 6 * order), jnp.bfloat16),
        ((sums_padded, 4 * species), jnp.bfloat16),
        ((species, width), f32),
        ((rows, width), f32),
        ((rows, width), f32),
    )
    return pl.pallas_call(
        functools.partial(transport_kernel, wide_count, narrow_count),
        out_shape=[jax.ShapeDtypeStruct(shape, dtype) for shape, dtype in outs],
        in_specs=[pl.BlockSpec(memory_space=pltpu.HBM)] * (3 + len(small)),
        out_specs=[vmem] * len(outs),
        scratch_shapes=[
            pltpu.VMEM((components, tall, columns), f32),
            pltpu.VMEM((tall, columns), f32),
            pltpu.VMEM((tall, columns), f32),
            *[pltpu.VMEM(array.shape, array.dtype) for array in small],
            pltpu.VMEM((2, packed, columns), f32),
            pltpu.VMEM((2, packed, columns), f32),
            pltpu.VMEM((narrow_count, components, rows, width), f32),
            pltpu.VMEM((species, 6 * order), f32),
            pltpu.VMEM((sums_padded, 4 * species), f32),
            pltpu.SemaphoreType.DMA((3 + len(small),)),
            pltpu.SemaphoreType.DMA((2,)),
            pltpu.SemaphoreType.DMA((2,)),
            pltpu.SemaphoreType.DMA((components, narrow_count - 1)),
            pltpu.SemaphoreType.DMA((components, narrow_count - 1)),
        ],
        compiler_params=pltpu.CompilerParams(
            collective_id=0, has_side_effects=True, vmem_limit_bytes=63 * 2**20
        ),
        name="transport",
    )(totals, courant, diffusion, *small)


def solve_spd(entry, right):
    order = len(right)
    lower, scaled, inverse = {}, {}, []
    start = 0
    while start < order:
        size = 2 if start < order // 2 else order - start
        block = range(start, start + size)
        work = {}
        for j in block:
            for i in range(j, order + 1):
                work[i, j] = right[j] if i == order else entry(i, j)
        for k in range(start):
            for i in range(start, order + 1):
                for j in block:
                    if i >= j:
                        work[i, j] = work[i, j] - lower[i, k] * scaled[j, k]
        for k in block:
            inverse.append(1.0 / work[k, k])
            for i in range(k + 1, order + 1):
                scaled[i, k] = work[i, k]
                lower[i, k] = work[i, k] * inverse[k]
            for j in range(k + 1, start + size):
                for i in range(j, order + 1):
                    work[i, j] = work[i, j] - lower[i, k] * scaled[j, k]
        start += size
    found = [lower[order, j] for j in range(order)]
    for i in reversed(range(order)):
        for j in range(i):
            found[j] = found[j] - lower[i, j] * found[i]
    return found


def newton_kernel(
    secondary_count,
    totals_ref,
    exponent_lhs,
    pair_lhs,
    offset_ref,
    on_ref,
    front_ref,
    out_ref,
    y_ref,
    sums_ref,
):
    order, group, width = totals_ref.shape
    pairs = order * (order + 1) // 2
    place = {}
    for i in range(order):
        for j in range(i, order):
            place[j, i] = len(place)

    for i in range(order):
        y_ref[i * group : (i + 1) * group, :] = jnp.log(totals_ref[i])
    offset = offset_ref[...]
    offset = jnp.concatenate([offset, offset], axis=1)

    def iterate(_, carry):
        for s in range(0, group, 2):
            y = jnp.concatenate(
                [y_ref[pl.ds(s + h, order, stride=group), :] for h in range(2)], axis=1
            )
            y1, y2, y3 = parts(y, 3)
            exponent = jnp.dot(
                exponent_lhs[...],
                jnp.concatenate([y1, y2, y1, y3, y1, y2], axis=0),
                preferred_element_type=jnp.float32,
            )
            x = jnp.exp(exponent + offset)
            on = jnp.concatenate([on_ref[s + h : s + h + 1, :] for h in range(2)], axis=1)
            x = jnp.concatenate([x[:secondary_count], x[secondary_count:] * on], axis=0)
            x1, x2 = parts(x, 2)
            sums = jnp.dot(
                pair_lhs[...],
                jnp.concatenate([x1, x2, x1, x2], axis=0),
                preferred_element_type=jnp.float32,
            )
            for h in range(2):
                sums_ref[pl.ds(s + h, pairs + order, stride=group), :] = sums[
                    : pairs + order, h * width : (h + 1) * width
                ]

        def total(p):
            return sums_ref[p * group : (p + 1) * group, :]

        old = [y_ref[i * group : (i + 1) * group, :] for i in range(order)]
        free = [jnp.exp(v) for v in old]
        residual = [free[i] + total(pairs + i) - totals_ref[i] for i in range(order)]

        def entry(i, j):
            value = total(place[i, j])
            return value + free[i] if i == j else value

        delta = solve_spd(entry, residual)
        largest = [jnp.abs(v) for v in delta]
        while len(largest) > 1:
            largest = [
                jnp.maximum(a, b) for a, b in zip(largest[::2], largest[1::2])
            ] + largest[len(largest) // 2 * 2 :]
        scale = 1.0 / jnp.maximum(largest[0], 1.0)
        for i in range(order):
            y_ref[i * group : (i + 1) * group, :] = y_ref[
                i * group : (i + 1) * group, :
            ] - delta[i] * scale
        return carry

    lax.fori_loop(0, ITERS, iterate, 0)

    front = front_ref[...] > 0.0
    for i in range(order):
        out_ref[i] = jnp.where(
            front, y_ref[i * group : (i + 1) * group, :], jnp.log(totals_ref[i])
        )


def speciate(totals, exponent_lhs, pair_lhs, offset, on, front, secondary_count):
    order, rows, width = totals.shape
    group = 8
    sums = order * (order + 1) // 2 + order
    whole = pl.BlockSpec(memory_space=pltpu.VMEM)
    block = pl.BlockSpec((order, group, width), lambda i: (0, i, 0))
    per_row = pl.BlockSpec((group, width), lambda i: (i, 0))
    return pl.pallas_call(
        functools.partial(newton_kernel, secondary_count),
        grid=(rows // group,),
        out_shape=jax.ShapeDtypeStruct(totals.shape, jnp.float32),
        in_specs=[block, whole, whole, whole, per_row, per_row],
        out_specs=block,
        scratch_shapes=[
            pltpu.VMEM((order * group, width), jnp.float32),
            pltpu.VMEM((sums * group, width), jnp.float32),
        ],
        compiler_params=pltpu.CompilerParams(vmem_limit_bytes=63 * 2**20),
        name="newton",
    )(totals, exponent_lhs, pair_lhs, offset, on, front)


def shards(
    totals,
    courant,
    diffusion,
    stoich,
    log_k,
    mineral_stoich,
    mineral_log_k,
    mineral_rate,
    front_counts,
    mineral_flags,
):
    moved = transport(
        totals,
        courant,
        diffusion,
        stoich,
        log_k,
        mineral_stoich,
        mineral_log_k,
        mineral_rate,
        front_counts,
        mineral_flags,
    )
    return speciate(*moved, stoich.shape[0])


def solution(mesh):
    placed = (
        P("narrow", "wide", None),
        P("wide", None),
        P("wide", None),
        P(),
        P(),
        P(),
        P(),
        P(),
        P(),
        P("wide", "narrow"),
    )
    return jax.shard_map(
        shards, mesh=mesh, in_specs=placed, out_specs=P(None, "wide", "narrow"), check_vma=False
    )
```

```python
import functools

import jax
import jax.numpy as jnp
from jax import lax
from jax.experimental import pallas as pl
from jax.experimental.pallas import tpu as pltpu
from jax.sharding import PartitionSpec as P

STEPS = 4
ITERS = 4
MESH = pl.DeviceIdType.MESH


def parts(values, count):
    found = []
    for _ in range(count):
        part = values.astype(jnp.bfloat16)
        found.append(part)
        values = values - part.astype(jnp.float32)
    return found


def column_of(row):
    count = row.shape[1]
    shape = (count, count)
    same = lax.broadcasted_iota(jnp.int32, shape, 0) == lax.broadcasted_iota(jnp.int32, shape, 1)
    return jnp.sum(jnp.where(same, jnp.broadcast_to(row, shape), 0.0), axis=1, keepdims=True)


def build_tables(stoich, log_k, mineral_stoich, mineral_log_k, mineral_rate, refs):
    exponent_out, pair_out, offset_out, wide_f32, pair_f32 = refs
    order = stoich.shape[0]
    species, width = offset_out.shape
    split, used = stoich.shape[1], stoich.shape[1] + mineral_stoich.shape[0]
    offset_out[...] = jnp.zeros_like(offset_out)
    offset_out[0:split, :] = jnp.broadcast_to(column_of(log_k[...]), (split, width))
    offset_out[split:used, :] = jnp.broadcast_to(
        column_of(jnp.log(mineral_rate[...]) - mineral_log_k[...]), (used - split, width)
    )

    def copies(length, first, period, lanes):
        row = lax.broadcasted_iota(jnp.int32, (length, lanes), 0) + first
        lane = lax.broadcasted_iota(jnp.int32, (length, lanes), 1)
        return jnp.where(lane % period == row, 1.0, 0.0).astype(jnp.float32)

    def product(left, right, dim):
        return lax.dot_general(
            left,
            right,
            (((dim,), (0,)), ((), ())),
            precision=lax.Precision.HIGHEST,
            preferred_element_type=jnp.float32,
        )

    spread = copies(order, 0, order, 6 * order)
    wide_f32[...] = jnp.zeros_like(wide_f32)
    wide_f32[0:split, :] = product(stoich[...], spread, 0)
    wide_f32[split:used, :] = product(mineral_stoich[...], spread, 1)
    wide = wide_f32[...]
    first, second, third = parts(wide, 3)
    lane = lax.broadcasted_iota(jnp.int32, wide.shape, 1) // order
    exponent_out[...] = jnp.where(
        jnp.logical_or(lane == 2, lane == 5),
        second.astype(jnp.float32),
        jnp.where(lane == 4, third.astype(jnp.float32), first.astype(jnp.float32)),
    ).astype(jnp.bfloat16)
    tall = product(stoich[...], copies(split, 0, species, 4 * species), 1) + product(
        mineral_stoich[...], copies(used - split, split, species, 4 * species), 0
    )
    pair_f32[...] = jnp.zeros_like(pair_f32)
    start = 0
    for i in range(order):
        pair_f32[start : start + order - i, :] = tall[i:order, :] * tall[i : i + 1, :]
        start += order - i
    pair_f32[start : start + order, :] = tall
    first, second = parts(pair_f32[...], 2)
    lane = lax.broadcasted_iota(jnp.int32, pair_f32.shape, 1)
    pair_out[...] = jnp.where(
        lane < 2 * species, first.astype(jnp.float32), second.astype(jnp.float32)
    ).astype(jnp.bfloat16)


def transport_kernel(
    wide_count,
    narrow_count,
    totals_any,
    courant_any,
    diffusion_any,
    stoich_any,
    log_k_any,
    mineral_stoich_any,
    mineral_log_k_any,
    mineral_rate_any,
    counts_any,
    flags_any,
    out_ref,
    exponent_out,
    pair_out,
    offset_out,
    on_out,
    front_out,
    tall_f,
    tall_c,
    tall_d,
    stoich,
    log_k,
    mineral_stoich,
    mineral_log_k,
    mineral_rate,
    counts,
    flags,
    halo_out,
    halo_in,
    staged,
    wide_f32,
    pair_f32,
    local_sem,
    halo_send,
    halo_recv,
    swap_send,
    swap_recv,
):
    components, tall, columns = tall_f.shape
    rows, width = out_ref.shape[1:]
    pad = (tall - rows) // 2
    wide = lax.axis_index("wide")
    narrow = lax.axis_index("narrow")
    has_above = wide > 0
    has_below = wide < wide_count - 1
    peers = [lax.rem(narrow + d, narrow_count) for d in range(1, narrow_count)]
    inside = pl.ds(pad, rows)

    moves = [
        pltpu.make_async_copy(src, dst, local_sem.at[k])
        for k, (src, dst) in enumerate(
            (
                (totals_any, tall_f.at[:, inside, :]),
                (courant_any, tall_c.at[inside, :]),
                (diffusion_any, tall_d.at[inside, :]),
                (stoich_any, stoich),
                (log_k_any, log_k),
                (mineral_stoich_any, mineral_stoich),
                (mineral_log_k_any, mineral_log_k),
                (mineral_rate_any, mineral_rate),
                (counts_any, counts),
                (flags_any, flags),
            )
        )
    ]
    for move in moves:
        move.start()

    barrier = pltpu.get_barrier_semaphore()
    for peer in peers:
        pl.semaphore_signal(barrier, inc=1, device_id=(wide, peer), device_id_type=MESH)

    @pl.when(has_above)
    def _():
        pl.semaphore_signal(barrier, inc=1, device_id=(wide - 1, narrow), device_id_type=MESH)

    @pl.when(has_below)
    def _():
        pl.semaphore_signal(barrier, inc=1, device_id=(wide + 1, narrow), device_id_type=MESH)

    for ref in (tall_c, tall_d):
        for start in (0, pad + rows):
            ref[start : start + pad, :] = jnp.zeros((pad, columns), jnp.float32)
    for start in (0, pad + rows):
        tall_f[:, start : start + pad, :] = jnp.zeros((components, pad, columns), jnp.float32)

    for move in moves[:3]:
        move.wait()

    for side, start in ((0, pad + rows - STEPS), (1, pad)):
        for c in range(components):
            halo_out[side, c * STEPS : (c + 1) * STEPS, :] = tall_f[c, start : start + STEPS, :]
        end = components * STEPS
        halo_out[side, end : end + STEPS, :] = tall_c[start : start + STEPS, :]
        halo_out[side, end + STEPS : end + 2 * STEPS, :] = tall_d[start : start + STEPS, :]

    neighbours = narrow_count - 1 + has_above.astype(jnp.int32) + has_below.astype(jnp.int32)
    pl.semaphore_wait(barrier, neighbours)

    def halo_copy(side, target):
        return pltpu.make_async_remote_copy(
            src_ref=halo_out.at[side],
            dst_ref=halo_in.at[side],
            send_sem=halo_send.at[side],
            recv_sem=halo_recv.at[side],
            device_id=(target, narrow),
            device_id_type=MESH,
        )

    to_below = halo_copy(0, wide + 1)
    to_above = halo_copy(1, wide - 1)

    @pl.when(has_below)
    def _():
        to_below.start()

    @pl.when(has_above)
    def _():
        to_above.start()

    swaps = []

    def advance(phase, start, length, offset, kept):
        part = pl.ds(start, length)
        courant, diffusion = tall_c[part, :], tall_d[part, :]
        keep = 1.0 - courant - 4.0 * diffusion
        push = courant + diffusion
        column = lax.broadcasted_iota(jnp.int32, (length, width), 1)
        first, last = column == 0, column == width - 1
        target = pl.ds(start + offset - pad, kept)
        for c in range(components):
            fields = tall_f[c, part, :]
            for _ in range(STEPS):
                upwind = pltpu.roll(fields, 1, 0)
                downwind = pltpu.roll(fields, length - 1, 0)
                left = pltpu.roll(fields, 1, 1)
                left = jnp.concatenate(
                    [jnp.where(first, 0.0, left[:, :width]), left[:, width:]], axis=1
                )
                right = pltpu.roll(fields, columns - 1, 1)
                right = jnp.concatenate(
                    [right[:, :-width], jnp.where(last, 0.0, right[:, -width:])], axis=1
                )
                fields = keep * fields + push * upwind + diffusion * (downwind + (left + right))
            for p in range(narrow_count):
                staged[p, c, target, :] = fields[
                    offset : offset + kept, p * width : (p + 1) * width
                ]
            for k, peer in enumerate(peers):
                copy = pltpu.make_async_remote_copy(
                    src_ref=staged.at[peer, c, target, :],
                    dst_ref=out_ref.at[narrow * components + c, target, :],
                    send_sem=swap_send.at[phase, c, k],
                    recv_sem=swap_recv.at[phase, c, k],
                    device_id=(wide, peer),
                    device_id_type=MESH,
                )
                copy.start()
                swaps.append(copy)
            out_ref[narrow * components + c, target, :] = staged[narrow, c, target, :]

    advance(0, pad, rows, pad, rows - 2 * pad)
    for move in moves[3:]:
        move.wait()
    build_tables(
        stoich,
        log_k,
        mineral_stoich,
        mineral_log_k,
        mineral_rate,
        (exponent_out, pair_out, offset_out, wide_f32, pair_f32),
    )
    blocks = flags.shape[1]
    row = lax.broadcasted_iota(jnp.int32, (rows, blocks), 0)
    mine = row // (rows // blocks) == lax.broadcasted_iota(jnp.int32, (rows, blocks), 1)
    flag_rows = jnp.broadcast_to(flags[...].astype(jnp.float32), (rows, blocks))
    on = jnp.sum(jnp.where(mine, flag_rows, 0.0), axis=1, keepdims=True)
    on_out[...] = jnp.broadcast_to(on, on_out.shape)
    row = lax.broadcasted_iota(jnp.int32, counts.shape, 0)
    lane = lax.broadcasted_iota(jnp.int32, counts.shape, 1)
    own = jnp.where(
        jnp.logical_and(row == narrow, lane == wide), counts[...].astype(jnp.float32), 0.0
    )
    own = jnp.sum(jnp.sum(own, axis=1, keepdims=True), axis=0, keepdims=True)
    row = lax.broadcasted_iota(jnp.int32, front_out.shape, 0) // (rows // blocks)
    front_out[...] = jnp.where(row.astype(jnp.float32) < own, 1.0, 0.0)

    def take(side, start):
        for c in range(components):
            tall_f[c, start : start + STEPS, :] = halo_in[side, c * STEPS : (c + 1) * STEPS, :]
        end = components * STEPS
        tall_c[start : start + STEPS, :] = halo_in[side, end : end + STEPS, :]
        tall_d[start : start + STEPS, :] = halo_in[side, end + STEPS : end + 2 * STEPS, :]

    @pl.when(has_above)
    def _():
        to_below.wait_recv()
        take(0, pad - STEPS)

    advance(1, 0, 3 * pad, pad, pad)

    @pl.when(has_below)
    def _():
        to_above.wait_recv()
        take(1, pad + rows)

    advance(2, rows - pad, 3 * pad, pad, pad)

    @pl.when(has_below)
    def _():
        to_below.wait_send()

    @pl.when(has_above)
    def _():
        to_above.wait_send()

    for copy in swaps:
        copy.wait()


def transport(
    totals,
    courant,
    diffusion,
    stoich,
    log_k,
    mineral_stoich,
    mineral_log_k,
    mineral_rate,
    front_counts,
    mineral_flags,
):
    components, rows, columns = totals.shape
    wide_count, narrow_count = lax.axis_size("wide"), lax.axis_size("narrow")
    width = columns // narrow_count
    order = components * narrow_count
    tall = rows + 2 * 8
    packed = (components + 2) * STEPS
    species = -(-(stoich.shape[0] + mineral_stoich.shape[0]) // 16) * 16
    sums = order * (order + 1) // 2 + order
    sums_padded = -(-sums // 16) * 16
    vmem = pl.BlockSpec(memory_space=pltpu.VMEM)
    small = (
        stoich.T,
        log_k.reshape(1, -1),
        mineral_stoich,
        mineral_log_k.reshape(1, -1),
        mineral_rate.reshape(1, -1),
        front_counts.T,
        mineral_flags.reshape(1, -1),
    )
    f32 = jnp.float32
    outs = (
        ((order, rows, width), f32),
        ((species, 6 * order), jnp.bfloat16),
        ((sums_padded, 4 * species), jnp.bfloat16),
        ((species, width), f32),
        ((rows, width), f32),
        ((rows, width), f32),
    )
    return pl.pallas_call(
        functools.partial(transport_kernel, wide_count, narrow_count),
        out_shape=[jax.ShapeDtypeStruct(shape, dtype) for shape, dtype in outs],
        in_specs=[pl.BlockSpec(memory_space=pltpu.HBM)] * (3 + len(small)),
        out_specs=[vmem] * len(outs),
        scratch_shapes=[
            pltpu.VMEM((components, tall, columns), f32),
            pltpu.VMEM((tall, columns), f32),
            pltpu.VMEM((tall, columns), f32),
            *[pltpu.VMEM(array.shape, array.dtype) for array in small],
            pltpu.VMEM((2, packed, columns), f32),
            pltpu.VMEM((2, packed, columns), f32),
            pltpu.VMEM((narrow_count, components, rows, width), f32),
            pltpu.VMEM((species, 6 * order), f32),
            pltpu.VMEM((sums_padded, 4 * species), f32),
            pltpu.SemaphoreType.DMA((3 + len(small),)),
            pltpu.SemaphoreType.DMA((2,)),
            pltpu.SemaphoreType.DMA((2,)),
            pltpu.SemaphoreType.DMA((3, components, narrow_count - 1)),
            pltpu.SemaphoreType.DMA((3, components, narrow_count - 1)),
        ],
        compiler_params=pltpu.CompilerParams(
            collective_id=0, has_side_effects=True, vmem_limit_bytes=63 * 2**20
        ),
        name="transport",
    )(totals, courant, diffusion, *small)


def reciprocal(value):
    guess = pl.reciprocal(value, approx=True)
    guess = guess * (2.0 - value * guess)
    return guess * (2.0 - value * guess)


def solve_spd(entry, right):
    order = len(right)
    lower, scaled, inverse = {}, {}, []
    start = 0
    while start < order:
        size = min(2, order - start)
        block = range(start, start + size)
        work = {}
        for j in block:
            for i in range(j, order + 1):
                work[i, j] = right[j] if i == order else entry(i, j)
        for k in range(start):
            for i in range(start, order + 1):
                for j in block:
                    if i >= j:
                        work[i, j] = work[i, j] - lower[i, k] * scaled[j, k]
        for k in block:
            inverse.append(reciprocal(work[k, k]))
            for i in range(k + 1, order + 1):
                scaled[i, k] = work[i, k]
                lower[i, k] = work[i, k] * inverse[k]
            for j in range(k + 1, start + size):
                for i in range(j, order + 1):
                    work[i, j] = work[i, j] - lower[i, k] * scaled[j, k]
        start += size
    found = [lower[order, j] for j in range(order)]
    for i in reversed(range(order)):
        for j in range(i):
            found[j] = found[j] - lower[i, j] * found[i]
    return found


def newton_kernel(
    secondary_count,
    totals_ref,
    exponent_lhs,
    pair_lhs,
    offset_ref,
    on_ref,
    front_ref,
    out_ref,
    y_ref,
    sums_ref,
):
    order, group, width = totals_ref.shape
    pairs = order * (order + 1) // 2
    place = {}
    for i in range(order):
        for j in range(i, order):
            place[j, i] = len(place)

    for i in range(order):
        y_ref[i * group : (i + 1) * group, :] = jnp.log(totals_ref[i])
    offset = offset_ref[...]
    offset = jnp.concatenate([offset, offset], axis=1)

    def iterate(_, carry):
        for s in range(0, group, 2):
            y = jnp.concatenate(
                [y_ref[pl.ds(s + h, order, stride=group), :] for h in range(2)], axis=1
            )
            y1, y2, y3 = parts(y, 3)
            exponent = jnp.dot(
                exponent_lhs[...],
                jnp.concatenate([y1, y2, y1, y3, y1, y2], axis=0),
                preferred_element_type=jnp.float32,
            )
            x = jnp.exp(exponent + offset)
            on = jnp.concatenate([on_ref[s + h : s + h + 1, :] for h in range(2)], axis=1)
            x = jnp.concatenate([x[:secondary_count], x[secondary_count:] * on], axis=0)
            x1, x2 = parts(x, 2)
            sums = jnp.dot(
                pair_lhs[...],
                jnp.concatenate([x1, x2, x1, x2], axis=0),
                preferred_element_type=jnp.float32,
            )
            for h in range(2):
                sums_ref[pl.ds(s + h, pairs + order, stride=group), :] = sums[
                    : pairs + order, h * width : (h + 1) * width
                ]

        def total(p):
            return sums_ref[p * group : (p + 1) * group, :]

        old = [y_ref[i * group : (i + 1) * group, :] for i in range(order)]
        free = [jnp.exp(v) for v in old]
        residual = [free[i] + total(pairs + i) - totals_ref[i] for i in range(order)]

        def entry(i, j):
            value = total(place[i, j])
            return value + free[i] if i == j else value

        delta = solve_spd(entry, residual)
        largest = [jnp.abs(v) for v in delta]
        while len(largest) > 1:
            largest = [
                jnp.maximum(a, b) for a, b in zip(largest[::2], largest[1::2])
            ] + largest[len(largest) // 2 * 2 :]
        scale = reciprocal(jnp.maximum(largest[0], 1.0))
        for i in range(order):
            y_ref[i * group : (i + 1) * group, :] = y_ref[
                i * group : (i + 1) * group, :
            ] - delta[i] * scale
        return carry

    lax.fori_loop(0, ITERS, iterate, 0)

    front = front_ref[...] > 0.0
    for i in range(order):
        out_ref[i] = jnp.where(
            front, y_ref[i * group : (i + 1) * group, :], jnp.log(totals_ref[i])
        )


def speciate(totals, exponent_lhs, pair_lhs, offset, on, front, secondary_count):
    order, rows, width = totals.shape
    group = 16
    sums = order * (order + 1) // 2 + order
    whole = pl.BlockSpec(memory_space=pltpu.VMEM)
    block = pl.BlockSpec((order, group, width), lambda i: (0, i, 0))
    per_row = pl.BlockSpec((group, width), lambda i: (i, 0))
    return pl.pallas_call(
        functools.partial(newton_kernel, secondary_count),
        grid=(rows // group,),
        out_shape=jax.ShapeDtypeStruct(totals.shape, jnp.float32),
        in_specs=[block, whole, whole, whole, per_row, per_row],
        out_specs=block,
        scratch_shapes=[
            pltpu.VMEM((order * group, width), jnp.float32),
            pltpu.VMEM((sums * group, width), jnp.float32),
        ],
        compiler_params=pltpu.CompilerParams(vmem_limit_bytes=63 * 2**20),
        name="newton",
    )(totals, exponent_lhs, pair_lhs, offset, on, front)


def shards(
    totals,
    courant,
    diffusion,
    stoich,
    log_k,
    mineral_stoich,
    mineral_log_k,
    mineral_rate,
    front_counts,
    mineral_flags,
):
    moved = transport(
        totals,
        courant,
        diffusion,
        stoich,
        log_k,
        mineral_stoich,
        mineral_log_k,
        mineral_rate,
        front_counts,
        mineral_flags,
    )
    return speciate(*moved, stoich.shape[0])


def solution(mesh):
    placed = (
        P("narrow", "wide", None),
        P("wide", None),
        P("wide", None),
        P(),
        P(),
        P(),
        P(),
        P(),
        P(),
        P("wide", "narrow"),
    )
    return jax.shard_map(
        shards, mesh=mesh, in_specs=placed, out_specs=P(None, "wide", "narrow"), check_vma=False
    )
```

```python
import functools

import jax
import jax.numpy as jnp
from jax import lax
from jax.experimental import pallas as pl
from jax.experimental.pallas import tpu as pltpu
from jax.sharding import PartitionSpec as P

STEPS = 4
ITERS = 4
MESH = pl.DeviceIdType.MESH


def parts(values, count):
    found = []
    for _ in range(count):
        part = values.astype(jnp.bfloat16)
        found.append(part)
        values = values - part.astype(jnp.float32)
    return found


def column_of(row):
    count = row.shape[1]
    shape = (count, count)
    same = lax.broadcasted_iota(jnp.int32, shape, 0) == lax.broadcasted_iota(jnp.int32, shape, 1)
    return jnp.sum(jnp.where(same, jnp.broadcast_to(row, shape), 0.0), axis=1, keepdims=True)


def build_tables(stoich, log_k, mineral_stoich, mineral_log_k, mineral_rate, refs):
    exponent_out, pair_out, offset_out, wide_f32, pair_f32 = refs
    order = stoich.shape[0]
    species, width = offset_out.shape
    split, used = stoich.shape[1], stoich.shape[1] + mineral_stoich.shape[0]
    offset_out[...] = jnp.zeros_like(offset_out)
    offset_out[0:split, :] = jnp.broadcast_to(column_of(log_k[...]), (split, width))
    offset_out[split:used, :] = jnp.broadcast_to(
        column_of(jnp.log(mineral_rate[...]) - mineral_log_k[...]), (used - split, width)
    )

    def copies(length, first, period, lanes):
        row = lax.broadcasted_iota(jnp.int32, (length, lanes), 0) + first
        lane = lax.broadcasted_iota(jnp.int32, (length, lanes), 1)
        return jnp.where(lane % period == row, 1.0, 0.0).astype(jnp.float32)

    def product(left, right, dim):
        return lax.dot_general(
            left,
            right,
            (((dim,), (0,)), ((), ())),
            precision=lax.Precision.HIGHEST,
            preferred_element_type=jnp.float32,
        )

    spread = copies(order, 0, order, 6 * order)
    wide_f32[...] = jnp.zeros_like(wide_f32)
    wide_f32[0:split, :] = product(stoich[...], spread, 0)
    wide_f32[split:used, :] = product(mineral_stoich[...], spread, 1)
    wide = wide_f32[...]
    first, second, third = parts(wide, 3)
    lane = lax.broadcasted_iota(jnp.int32, wide.shape, 1) // order
    exponent_out[...] = jnp.where(
        jnp.logical_or(lane == 2, lane == 5),
        second.astype(jnp.float32),
        jnp.where(lane == 4, third.astype(jnp.float32), first.astype(jnp.float32)),
    ).astype(jnp.bfloat16)
    tall = product(stoich[...], copies(split, 0, species, 4 * species), 1) + product(
        mineral_stoich[...], copies(used - split, split, species, 4 * species), 0
    )
    pair_f32[...] = jnp.zeros_like(pair_f32)
    start = 0
    for i in range(order):
        pair_f32[start : start + order - i, :] = tall[i:order, :] * tall[i : i + 1, :]
        start += order - i
    pair_f32[start : start + order, :] = tall
    first, second = parts(pair_f32[...], 2)
    lane = lax.broadcasted_iota(jnp.int32, pair_f32.shape, 1)
    pair_out[...] = jnp.where(
        lane < 2 * species, first.astype(jnp.float32), second.astype(jnp.float32)
    ).astype(jnp.bfloat16)


def transport_kernel(
    wide_count,
    narrow_count,
    totals_any,
    courant_any,
    diffusion_any,
    stoich_any,
    log_k_any,
    mineral_stoich_any,
    mineral_log_k_any,
    mineral_rate_any,
    counts_any,
    flags_any,
    out_ref,
    exponent_out,
    pair_out,
    offset_out,
    on_out,
    front_out,
    tall_f,
    tall_c,
    tall_d,
    stoich,
    log_k,
    mineral_stoich,
    mineral_log_k,
    mineral_rate,
    counts,
    flags,
    halo_out,
    halo_in,
    staged,
    wide_f32,
    pair_f32,
    local_sem,
    halo_send,
    halo_recv,
    swap_send,
    swap_recv,
):
    components, tall, columns = tall_f.shape
    rows, width = out_ref.shape[1:]
    pad = (tall - rows) // 2
    wide = lax.axis_index("wide")
    narrow = lax.axis_index("narrow")
    has_above = wide > 0
    has_below = wide < wide_count - 1
    peers = [lax.rem(narrow + d, narrow_count) for d in range(1, narrow_count)]
    inside = pl.ds(pad, rows)

    moves = [
        pltpu.make_async_copy(src, dst, local_sem.at[k])
        for k, (src, dst) in enumerate(
            (
                (totals_any, tall_f.at[:, inside, :]),
                (courant_any, tall_c.at[inside, :]),
                (diffusion_any, tall_d.at[inside, :]),
                (stoich_any, stoich),
                (log_k_any, log_k),
                (mineral_stoich_any, mineral_stoich),
                (mineral_log_k_any, mineral_log_k),
                (mineral_rate_any, mineral_rate),
                (counts_any, counts),
                (flags_any, flags),
            )
        )
    ]
    for move in moves:
        move.start()

    barrier = pltpu.get_barrier_semaphore()
    for peer in peers:
        pl.semaphore_signal(barrier, inc=1, device_id=(wide, peer), device_id_type=MESH)

    @pl.when(has_above)
    def _():
        pl.semaphore_signal(barrier, inc=1, device_id=(wide - 1, narrow), device_id_type=MESH)

    @pl.when(has_below)
    def _():
        pl.semaphore_signal(barrier, inc=1, device_id=(wide + 1, narrow), device_id_type=MESH)

    for ref in (tall_c, tall_d):
        for start in (0, pad + rows):
            ref[start : start + pad, :] = jnp.zeros((pad, columns), jnp.float32)
    for start in (0, pad + rows):
        tall_f[:, start : start + pad, :] = jnp.zeros((components, pad, columns), jnp.float32)

    for move in moves[:3]:
        move.wait()

    for side, start in ((0, pad + rows - STEPS), (1, pad)):
        for c in range(components):
            halo_out[side, c * STEPS : (c + 1) * STEPS, :] = tall_f[c, start : start + STEPS, :]
        end = components * STEPS
        halo_out[side, end : end + STEPS, :] = tall_c[start : start + STEPS, :]
        halo_out[side, end + STEPS : end + 2 * STEPS, :] = tall_d[start : start + STEPS, :]

    neighbours = narrow_count - 1 + has_above.astype(jnp.int32) + has_below.astype(jnp.int32)
    pl.semaphore_wait(barrier, neighbours)

    def halo_copy(side, target):
        return pltpu.make_async_remote_copy(
            src_ref=halo_out.at[side],
            dst_ref=halo_in.at[side],
            send_sem=halo_send.at[side],
            recv_sem=halo_recv.at[side],
            device_id=(target, narrow),
            device_id_type=MESH,
        )

    to_below = halo_copy(0, wide + 1)
    to_above = halo_copy(1, wide - 1)

    @pl.when(has_below)
    def _():
        to_below.start()

    @pl.when(has_above)
    def _():
        to_above.start()

    swaps = []

    def advance(phase, start, length, offset, kept):
        part = pl.ds(start, length)
        courant, diffusion = tall_c[part, :], tall_d[part, :]
        keep = 1.0 - courant - 4.0 * diffusion
        push = courant + diffusion
        column = lax.broadcasted_iota(jnp.int32, (length, width), 1)
        first, last = column == 0, column == width - 1
        target = pl.ds(start + offset - pad, kept)
        for c in range(components):
            fields = tall_f[c, part, :]
            for _ in range(STEPS):
                upwind = pltpu.roll(fields, 1, 0)
                downwind = pltpu.roll(fields, length - 1, 0)
                left = pltpu.roll(fields, 1, 1)
                left = jnp.concatenate(
                    [jnp.where(first, 0.0, left[:, :width]), left[:, width:]], axis=1
                )
                right = pltpu.roll(fields, columns - 1, 1)
                right = jnp.concatenate(
                    [right[:, :-width], jnp.where(last, 0.0, right[:, -width:])], axis=1
                )
                fields = keep * fields + push * upwind + diffusion * (downwind + (left + right))
            for p in range(narrow_count):
                staged[p, c, target, :] = fields[
                    offset : offset + kept, p * width : (p + 1) * width
                ]
            for k, peer in enumerate(peers):
                copy = pltpu.make_async_remote_copy(
                    src_ref=staged.at[peer, c, target, :],
                    dst_ref=out_ref.at[narrow * components + c, target, :],
                    send_sem=swap_send.at[phase, c, k],
                    recv_sem=swap_recv.at[phase, c, k],
                    device_id=(wide, peer),
                    device_id_type=MESH,
                )
                copy.start()
                swaps.append(copy)
            out_ref[narrow * components + c, target, :] = staged[narrow, c, target, :]

    advance(0, pad, rows, pad, rows - 2 * pad)
    def take(side, start):
        for c in range(components):
            tall_f[c, start : start + STEPS, :] = halo_in[side, c * STEPS : (c + 1) * STEPS, :]
        end = components * STEPS
        tall_c[start : start + STEPS, :] = halo_in[side, end : end + STEPS, :]
        tall_d[start : start + STEPS, :] = halo_in[side, end + STEPS : end + 2 * STEPS, :]

    @pl.when(has_above)
    def _():
        to_below.wait_recv()
        take(0, pad - STEPS)

    advance(1, 0, 3 * pad, pad, pad)

    @pl.when(has_below)
    def _():
        to_above.wait_recv()
        take(1, pad + rows)

    advance(2, rows - pad, 3 * pad, pad, pad)

    for move in moves[3:]:
        move.wait()
    build_tables(
        stoich,
        log_k,
        mineral_stoich,
        mineral_log_k,
        mineral_rate,
        (exponent_out, pair_out, offset_out, wide_f32, pair_f32),
    )
    blocks = flags.shape[1]
    row = lax.broadcasted_iota(jnp.int32, (rows, blocks), 0)
    mine = row // (rows // blocks) == lax.broadcasted_iota(jnp.int32, (rows, blocks), 1)
    flag_rows = jnp.broadcast_to(flags[...].astype(jnp.float32), (rows, blocks))
    on = jnp.sum(jnp.where(mine, flag_rows, 0.0), axis=1, keepdims=True)
    on_out[...] = jnp.broadcast_to(on, on_out.shape)
    row = lax.broadcasted_iota(jnp.int32, counts.shape, 0)
    lane = lax.broadcasted_iota(jnp.int32, counts.shape, 1)
    own = jnp.where(
        jnp.logical_and(row == narrow, lane == wide), counts[...].astype(jnp.float32), 0.0
    )
    own = jnp.sum(jnp.sum(own, axis=1, keepdims=True), axis=0, keepdims=True)
    row = lax.broadcasted_iota(jnp.int32, front_out.shape, 0) // (rows // blocks)
    front_out[...] = jnp.where(row.astype(jnp.float32) < own, 1.0, 0.0)

    @pl.when(has_below)
    def _():
        to_below.wait_send()

    @pl.when(has_above)
    def _():
        to_above.wait_send()

    for copy in swaps:
        copy.wait()


def transport(
    totals,
    courant,
    diffusion,
    stoich,
    log_k,
    mineral_stoich,
    mineral_log_k,
    mineral_rate,
    front_counts,
    mineral_flags,
):
    components, rows, columns = totals.shape
    wide_count, narrow_count = lax.axis_size("wide"), lax.axis_size("narrow")
    width = columns // narrow_count
    order = components * narrow_count
    tall = rows + 2 * 8
    packed = (components + 2) * STEPS
    species = -(-(stoich.shape[0] + mineral_stoich.shape[0]) // 16) * 16
    sums = order * (order + 1) // 2 + order
    sums_padded = -(-sums // 16) * 16
    vmem = pl.BlockSpec(memory_space=pltpu.VMEM)
    small = (
        stoich.T,
        log_k.reshape(1, -1),
        mineral_stoich,
        mineral_log_k.reshape(1, -1),
        mineral_rate.reshape(1, -1),
        front_counts.T,
        mineral_flags.reshape(1, -1),
    )
    f32 = jnp.float32
    outs = (
        ((order, rows, width), f32),
        ((species, 6 * order), jnp.bfloat16),
        ((sums_padded, 4 * species), jnp.bfloat16),
        ((species, width), f32),
        ((rows, width), f32),
        ((rows, width), f32),
    )
    return pl.pallas_call(
        functools.partial(transport_kernel, wide_count, narrow_count),
        out_shape=[jax.ShapeDtypeStruct(shape, dtype) for shape, dtype in outs],
        in_specs=[pl.BlockSpec(memory_space=pltpu.HBM)] * (3 + len(small)),
        out_specs=[vmem] * len(outs),
        scratch_shapes=[
            pltpu.VMEM((components, tall, columns), f32),
            pltpu.VMEM((tall, columns), f32),
            pltpu.VMEM((tall, columns), f32),
            *[pltpu.VMEM(array.shape, array.dtype) for array in small],
            pltpu.VMEM((2, packed, columns), f32),
            pltpu.VMEM((2, packed, columns), f32),
            pltpu.VMEM((narrow_count, components, rows, width), f32),
            pltpu.VMEM((species, 6 * order), f32),
            pltpu.VMEM((sums_padded, 4 * species), f32),
            pltpu.SemaphoreType.DMA((3 + len(small),)),
            pltpu.SemaphoreType.DMA((2,)),
            pltpu.SemaphoreType.DMA((2,)),
            pltpu.SemaphoreType.DMA((3, components, narrow_count - 1)),
            pltpu.SemaphoreType.DMA((3, components, narrow_count - 1)),
        ],
        compiler_params=pltpu.CompilerParams(
            collective_id=0, has_side_effects=True, vmem_limit_bytes=63 * 2**20
        ),
        name="transport",
    )(totals, courant, diffusion, *small)


def reciprocal(value):
    guess = pl.reciprocal(value, approx=True)
    guess = guess * (2.0 - value * guess)
    return guess * (2.0 - value * guess)


def solve_spd(entry, right):
    order = len(right)
    lower, scaled, inverse = {}, {}, []
    start = 0
    while start < order:
        size = min(2, order - start)
        block = range(start, start + size)
        work = {}
        for j in block:
            for i in range(j, order + 1):
                work[i, j] = right[j] if i == order else entry(i, j)
        for k in range(start):
            for i in range(start, order + 1):
                for j in block:
                    if i >= j:
                        work[i, j] = work[i, j] - lower[i, k] * scaled[j, k]
        for k in block:
            inverse.append(reciprocal(work[k, k]))
            for i in range(k + 1, order + 1):
                scaled[i, k] = work[i, k]
                lower[i, k] = work[i, k] * inverse[k]
            for j in range(k + 1, start + size):
                for i in range(j, order + 1):
                    work[i, j] = work[i, j] - lower[i, k] * scaled[j, k]
        start += size
        yield
    found = [lower[order, j] for j in range(order)]
    for i in reversed(range(order)):
        for j in range(i):
            found[j] = found[j] - lower[i, j] * found[i]
        if i % 4 == 0:
            yield
    return found


def together(*runs):
    runs = list(runs)
    while runs:
        runs = [run for run in runs if next(run, runs) is not runs]


def newton_kernel(
    secondary_count,
    totals_ref,
    exponent_lhs,
    pair_lhs,
    offset_ref,
    on_ref,
    front_ref,
    out_ref,
    *scratch,
):
    order, rows, width = totals_ref.shape
    group = rows // 2
    pairs = order * (order + 1) // 2
    place = {}
    for i in range(order):
        for j in range(i, order):
            place[j, i] = len(place)
    offset = offset_ref[...]
    offset = jnp.concatenate([offset, offset], axis=1)

    def total_of(base, i):
        return totals_ref[i, base : base + group, :]

    def sum_steps(base, y_ref, sums_ref):
        for s in range(0, group, 2):
            y = jnp.concatenate(
                [y_ref[pl.ds(s + h, order, stride=group), :] for h in range(2)], axis=1
            )
            y1, y2, y3 = parts(y, 3)
            exponent = jnp.dot(
                exponent_lhs[...],
                jnp.concatenate([y1, y2, y1, y3, y1, y2], axis=0),
                preferred_element_type=jnp.float32,
            )
            yield
            x = jnp.exp(exponent + offset)
            on = jnp.concatenate(
                [on_ref[base + s + h : base + s + h + 1, :] for h in range(2)], axis=1
            )
            x = jnp.concatenate([x[:secondary_count], x[secondary_count:] * on], axis=0)
            x1, x2 = parts(x, 2)
            sums = jnp.dot(
                pair_lhs[...],
                jnp.concatenate([x1, x2, x1, x2], axis=0),
                preferred_element_type=jnp.float32,
            )
            for h in range(2):
                sums_ref[pl.ds(s + h, pairs + order, stride=group), :] = sums[
                    : pairs + order, h * width : (h + 1) * width
                ]
            yield

    def update_steps(base, y_ref, sums_ref):
        def total(p):
            return sums_ref[p * group : (p + 1) * group, :]

        free = [jnp.exp(y_ref[i * group : (i + 1) * group, :]) for i in range(order)]
        residual = [free[i] + total(pairs + i) - total_of(base, i) for i in range(order)]

        def entry(i, j):
            value = total(place[i, j])
            return value + free[i] if i == j else value

        delta = yield from solve_spd(entry, residual)
        largest = [jnp.abs(v) for v in delta]
        while len(largest) > 1:
            largest = [jnp.maximum(a, b) for a, b in zip(largest[::2], largest[1::2])] + largest[
                len(largest) // 2 * 2 :
            ]
        scale = reciprocal(jnp.maximum(largest[0], 1.0))
        for i in range(order):
            part = slice(i * group, (i + 1) * group)
            y_ref[part, :] = y_ref[part, :] - delta[i] * scale

    early = (0, scratch[0], scratch[1])
    late = (group, scratch[2], scratch[3])
    for base, y_ref, _ in (early, late):
        for i in range(order):
            y_ref[i * group : (i + 1) * group, :] = jnp.log(total_of(base, i))
    together(sum_steps(*early))

    def iterate(_, carry):
        together(update_steps(*early), sum_steps(*late))
        together(update_steps(*late), sum_steps(*early))
        return carry

    lax.fori_loop(0, ITERS, iterate, 0)

    for base, y_ref, _ in (early, late):
        front = front_ref[base : base + group, :] > 0.0
        for i in range(order):
            out_ref[i, base : base + group, :] = jnp.where(
                front, y_ref[i * group : (i + 1) * group, :], jnp.log(total_of(base, i))
            )


def speciate(totals, exponent_lhs, pair_lhs, offset, on, front, secondary_count):
    order, rows, width = totals.shape
    group = 16
    sums = order * (order + 1) // 2 + order
    whole = pl.BlockSpec(memory_space=pltpu.VMEM)
    block = pl.BlockSpec((order, group, width), lambda i: (0, i, 0))
    per_row = pl.BlockSpec((group, width), lambda i: (i, 0))
    return pl.pallas_call(
        functools.partial(newton_kernel, secondary_count),
        grid=(rows // group,),
        out_shape=jax.ShapeDtypeStruct(totals.shape, jnp.float32),
        in_specs=[block, whole, whole, whole, per_row, per_row],
        out_specs=block,
        scratch_shapes=[
            pltpu.VMEM((order * group // 2, width), jnp.float32),
            pltpu.VMEM((sums * group // 2, width), jnp.float32),
        ]
        * 2,
        compiler_params=pltpu.CompilerParams(vmem_limit_bytes=63 * 2**20),
        name="newton",
    )(totals, exponent_lhs, pair_lhs, offset, on, front)


def shards(
    totals,
    courant,
    diffusion,
    stoich,
    log_k,
    mineral_stoich,
    mineral_log_k,
    mineral_rate,
    front_counts,
    mineral_flags,
):
    moved = transport(
        totals,
        courant,
        diffusion,
        stoich,
        log_k,
        mineral_stoich,
        mineral_log_k,
        mineral_rate,
        front_counts,
        mineral_flags,
    )
    return speciate(*moved, stoich.shape[0])


def solution(mesh):
    placed = (
        P("narrow", "wide", None),
        P("wide", None),
        P("wide", None),
        P(),
        P(),
        P(),
        P(),
        P(),
        P(),
        P("wide", "narrow"),
    )
    return jax.shard_map(
        shards, mesh=mesh, in_specs=placed, out_specs=P(None, "wide", "narrow"), check_vma=False
    )
```

```python
import functools

import jax
import jax.numpy as jnp
from jax import lax
from jax.experimental import pallas as pl
from jax.experimental.pallas import tpu as pltpu
from jax.sharding import PartitionSpec as P

STEPS = 4
ITERS = 4
MESH = pl.DeviceIdType.MESH


def parts(values, count):
    found = []
    for _ in range(count):
        part = values.astype(jnp.bfloat16)
        found.append(part)
        values = values - part.astype(jnp.float32)
    return found


def column_of(row):
    count = row.shape[1]
    shape = (count, count)
    same = lax.broadcasted_iota(jnp.int32, shape, 0) == lax.broadcasted_iota(jnp.int32, shape, 1)
    return jnp.sum(jnp.where(same, jnp.broadcast_to(row, shape), 0.0), axis=1, keepdims=True)


def build_tables(stoich, log_k, mineral_stoich, mineral_log_k, mineral_rate, refs):
    exponent_out, pair_out, offset_out, wide_f32, pair_f32 = refs
    order = stoich.shape[0]
    species, width = offset_out.shape
    split, used = stoich.shape[1], stoich.shape[1] + mineral_stoich.shape[0]
    offset_out[...] = jnp.zeros_like(offset_out)
    offset_out[0:split, :] = jnp.broadcast_to(column_of(log_k[...]), (split, width))
    offset_out[split:used, :] = jnp.broadcast_to(
        column_of(jnp.log(mineral_rate[...]) - mineral_log_k[...]), (used - split, width)
    )

    def copies(length, first, period, lanes):
        row = lax.broadcasted_iota(jnp.int32, (length, lanes), 0) + first
        lane = lax.broadcasted_iota(jnp.int32, (length, lanes), 1)
        return jnp.where(lane % period == row, 1.0, 0.0).astype(jnp.float32)

    def product(left, right, dim):
        return lax.dot_general(
            left,
            right,
            (((dim,), (0,)), ((), ())),
            precision=lax.Precision.HIGHEST,
            preferred_element_type=jnp.float32,
        )

    spread = copies(order, 0, order, 6 * order)
    wide_f32[...] = jnp.zeros_like(wide_f32)
    wide_f32[0:split, :] = product(stoich[...], spread, 0)
    wide_f32[split:used, :] = product(mineral_stoich[...], spread, 1)
    wide = wide_f32[...]
    first, second, third = parts(wide, 3)
    lane = lax.broadcasted_iota(jnp.int32, wide.shape, 1) // order
    exponent_out[...] = jnp.where(
        jnp.logical_or(lane == 2, lane == 5),
        second.astype(jnp.float32),
        jnp.where(lane == 4, third.astype(jnp.float32), first.astype(jnp.float32)),
    ).astype(jnp.bfloat16)
    tall = product(stoich[...], copies(split, 0, species, 4 * species), 1) + product(
        mineral_stoich[...], copies(used - split, split, species, 4 * species), 0
    )
    pair_f32[...] = jnp.zeros_like(pair_f32)
    start = 0
    for i in range(order):
        pair_f32[start : start + order - i, :] = tall[i:order, :] * tall[i : i + 1, :]
        start += order - i
    pair_f32[start : start + order, :] = tall
    first, second = parts(pair_f32[...], 2)
    lane = lax.broadcasted_iota(jnp.int32, pair_f32.shape, 1)
    pair_out[...] = jnp.where(
        lane < 2 * species, first.astype(jnp.float32), second.astype(jnp.float32)
    ).astype(jnp.bfloat16)


def transport_kernel(
    wide_count,
    narrow_count,
    totals_any,
    courant_any,
    diffusion_any,
    stoich_any,
    log_k_any,
    mineral_stoich_any,
    mineral_log_k_any,
    mineral_rate_any,
    counts_any,
    flags_any,
    out_ref,
    exponent_out,
    pair_out,
    offset_out,
    on_out,
    front_out,
    tall_f,
    tall_c,
    tall_d,
    stoich,
    log_k,
    mineral_stoich,
    mineral_log_k,
    mineral_rate,
    counts,
    flags,
    halo_out,
    halo_in,
    staged,
    wide_f32,
    pair_f32,
    local_sem,
    halo_send,
    halo_recv,
    swap_send,
    swap_recv,
):
    components, tall, columns = tall_f.shape
    rows, width = out_ref.shape[1:]
    pad = (tall - rows) // 2
    wide = lax.axis_index("wide")
    narrow = lax.axis_index("narrow")
    has_above = wide > 0
    has_below = wide < wide_count - 1
    peers = [lax.rem(narrow + d, narrow_count) for d in range(1, narrow_count)]
    inside = pl.ds(pad, rows)

    moves = [
        pltpu.make_async_copy(src, dst, local_sem.at[k])
        for k, (src, dst) in enumerate(
            (
                (courant_any, tall_c.at[inside, :]),
                (diffusion_any, tall_d.at[inside, :]),
                *[
                    (
                        totals_any.at[:, pl.ds(start, length), :],
                        tall_f.at[:, pl.ds(pad + start, length), :],
                    )
                    for start, length in ((0, pad), (rows - pad, pad), (pad, rows - 2 * pad))
                ],
                (stoich_any, stoich),
                (log_k_any, log_k),
                (mineral_stoich_any, mineral_stoich),
                (mineral_log_k_any, mineral_log_k),
                (mineral_rate_any, mineral_rate),
                (counts_any, counts),
                (flags_any, flags),
            )
        )
    ]
    for move in moves:
        move.start()

    barrier = pltpu.get_barrier_semaphore()
    for peer in peers:
        pl.semaphore_signal(barrier, inc=1, device_id=(wide, peer), device_id_type=MESH)

    @pl.when(has_above)
    def _():
        pl.semaphore_signal(barrier, inc=1, device_id=(wide - 1, narrow), device_id_type=MESH)

    @pl.when(has_below)
    def _():
        pl.semaphore_signal(barrier, inc=1, device_id=(wide + 1, narrow), device_id_type=MESH)

    for ref in (tall_c, tall_d):
        for start in (0, pad + rows):
            ref[start : start + pad, :] = jnp.zeros((pad, columns), jnp.float32)
    for start in (0, pad + rows):
        tall_f[:, start : start + pad, :] = jnp.zeros((components, pad, columns), jnp.float32)

    for move in moves[:4]:
        move.wait()

    for side, start in ((0, pad + rows - STEPS), (1, pad)):
        halo_out[side, 0:STEPS, :] = tall_c[start : start + STEPS, :]
        halo_out[side, STEPS : 2 * STEPS, :] = tall_d[start : start + STEPS, :]
        for c in range(components):
            at = (c + 2) * STEPS
            halo_out[side, at : at + STEPS, :] = tall_f[c, start : start + STEPS, :]

    neighbours = narrow_count - 1 + has_above.astype(jnp.int32) + has_below.astype(jnp.int32)
    pl.semaphore_wait(barrier, neighbours)

    messages = halo_out.shape[1] // pad

    def halo_copies(side, target):
        return [
            pltpu.make_async_remote_copy(
                src_ref=halo_out.at[side, pl.ds(m * pad, pad), :],
                dst_ref=halo_in.at[side, pl.ds(m * pad, pad), :],
                send_sem=halo_send.at[side, m],
                recv_sem=halo_recv.at[side, m],
                device_id=(target, narrow),
                device_id_type=MESH,
            )
            for m in range(messages)
        ]

    to_below = halo_copies(0, wide + 1)
    to_above = halo_copies(1, wide - 1)

    @pl.when(has_below)
    def _():
        for copy in to_below:
            copy.start()

    @pl.when(has_above)
    def _():
        for copy in to_above:
            copy.start()

    moves[4].wait()
    swaps = []

    def advance(phase, chosen, start, length, offset, kept):
        part = pl.ds(start, length)
        courant, diffusion = tall_c[part, :], tall_d[part, :]
        keep = 1.0 - courant - 4.0 * diffusion
        push = courant + diffusion
        column = lax.broadcasted_iota(jnp.int32, (length, width), 1)
        first, last = column == 0, column == width - 1
        target = pl.ds(start + offset - pad, kept)
        for c in chosen:
            fields = tall_f[c, part, :]
            for _ in range(STEPS):
                upwind = pltpu.roll(fields, 1, 0)
                downwind = pltpu.roll(fields, length - 1, 0)
                left = pltpu.roll(fields, 1, 1)
                left = jnp.concatenate(
                    [jnp.where(first, 0.0, left[:, :width]), left[:, width:]], axis=1
                )
                right = pltpu.roll(fields, columns - 1, 1)
                right = jnp.concatenate(
                    [right[:, :-width], jnp.where(last, 0.0, right[:, -width:])], axis=1
                )
                fields = keep * fields + push * upwind + diffusion * (downwind + (left + right))
            for p in range(narrow_count):
                staged[p, c, target, :] = fields[
                    offset : offset + kept, p * width : (p + 1) * width
                ]
            for k, peer in enumerate(peers):
                copy = pltpu.make_async_remote_copy(
                    src_ref=staged.at[peer, c, target, :],
                    dst_ref=out_ref.at[narrow * components + c, target, :],
                    send_sem=swap_send.at[phase, c, k],
                    recv_sem=swap_recv.at[phase, c, k],
                    device_id=(wide, peer),
                    device_id_type=MESH,
                )
                copy.start()
                swaps.append(copy)
            out_ref[narrow * components + c, target, :] = staged[narrow, c, target, :]

    advance(0, range(components), pad, rows, pad, rows - 2 * pad)
    per = pad // STEPS

    def take(side, m, start):
        part = slice(start, start + STEPS)
        if m == 0:
            tall_c[part, :] = halo_in[side, 0:STEPS, :]
            tall_d[part, :] = halo_in[side, STEPS : 2 * STEPS, :]
        else:
            for k in range(per):
                at = m * pad + k * STEPS
                tall_f[(m - 1) * per + k, part, :] = halo_in[side, at : at + STEPS, :]

    for m in range(messages):

        @pl.when(has_above)
        def _():
            to_below[m].wait_recv()
            take(0, m, pad - STEPS)

        @pl.when(has_below)
        def _():
            to_above[m].wait_recv()
            take(1, m, pad + rows)

        if m > 0:
            chosen = range((m - 1) * per, m * per)
            advance(1, chosen, pad - STEPS, 2 * pad, STEPS, pad)
            advance(2, chosen, rows - STEPS, 2 * pad, STEPS, pad)

    for move in moves[5:]:
        move.wait()
    build_tables(
        stoich,
        log_k,
        mineral_stoich,
        mineral_log_k,
        mineral_rate,
        (exponent_out, pair_out, offset_out, wide_f32, pair_f32),
    )
    blocks = flags.shape[1]
    row = lax.broadcasted_iota(jnp.int32, (rows, blocks), 0)
    mine = row // (rows // blocks) == lax.broadcasted_iota(jnp.int32, (rows, blocks), 1)
    flag_rows = jnp.broadcast_to(flags[...].astype(jnp.float32), (rows, blocks))
    on = jnp.sum(jnp.where(mine, flag_rows, 0.0), axis=1, keepdims=True)
    on_out[...] = jnp.broadcast_to(on, on_out.shape)
    row = lax.broadcasted_iota(jnp.int32, counts.shape, 0)
    lane = lax.broadcasted_iota(jnp.int32, counts.shape, 1)
    own = jnp.where(
        jnp.logical_and(row == narrow, lane == wide), counts[...].astype(jnp.float32), 0.0
    )
    own = jnp.sum(jnp.sum(own, axis=1, keepdims=True), axis=0, keepdims=True)
    row = lax.broadcasted_iota(jnp.int32, front_out.shape, 0) // (rows // blocks)
    front_out[...] = jnp.where(row.astype(jnp.float32) < own, 1.0, 0.0)

    @pl.when(has_below)
    def _():
        for copy in to_below:
            copy.wait_send()

    @pl.when(has_above)
    def _():
        for copy in to_above:
            copy.wait_send()

    for copy in swaps:
        copy.wait()


def transport(
    totals,
    courant,
    diffusion,
    stoich,
    log_k,
    mineral_stoich,
    mineral_log_k,
    mineral_rate,
    front_counts,
    mineral_flags,
):
    components, rows, columns = totals.shape
    wide_count, narrow_count = lax.axis_size("wide"), lax.axis_size("narrow")
    width = columns // narrow_count
    order = components * narrow_count
    tall = rows + 2 * 8
    packed = (components + 2) * STEPS
    species = -(-(stoich.shape[0] + mineral_stoich.shape[0]) // 16) * 16
    sums = order * (order + 1) // 2 + order
    sums_padded = -(-sums // 16) * 16
    vmem = pl.BlockSpec(memory_space=pltpu.VMEM)
    small = (
        stoich.T,
        log_k.reshape(1, -1),
        mineral_stoich,
        mineral_log_k.reshape(1, -1),
        mineral_rate.reshape(1, -1),
        front_counts.T,
        mineral_flags.reshape(1, -1),
    )
    f32 = jnp.float32
    outs = (
        ((order, rows, width), f32),
        ((species, 6 * order), jnp.bfloat16),
        ((sums_padded, 4 * species), jnp.bfloat16),
        ((species, width), f32),
        ((rows, width), f32),
        ((rows, width), f32),
    )
    return pl.pallas_call(
        functools.partial(transport_kernel, wide_count, narrow_count),
        out_shape=[jax.ShapeDtypeStruct(shape, dtype) for shape, dtype in outs],
        in_specs=[pl.BlockSpec(memory_space=pltpu.HBM)] * (3 + len(small)),
        out_specs=[vmem] * len(outs),
        scratch_shapes=[
            pltpu.VMEM((components, tall, columns), f32),
            pltpu.VMEM((tall, columns), f32),
            pltpu.VMEM((tall, columns), f32),
            *[pltpu.VMEM(array.shape, array.dtype) for array in small],
            pltpu.VMEM((2, packed, columns), f32),
            pltpu.VMEM((2, packed, columns), f32),
            pltpu.VMEM((narrow_count, components, rows, width), f32),
            pltpu.VMEM((species, 6 * order), f32),
            pltpu.VMEM((sums_padded, 4 * species), f32),
            pltpu.SemaphoreType.DMA((5 + len(small),)),
            pltpu.SemaphoreType.DMA((2, packed // 8)),
            pltpu.SemaphoreType.DMA((2, packed // 8)),
            pltpu.SemaphoreType.DMA((3, components, narrow_count - 1)),
            pltpu.SemaphoreType.DMA((3, components, narrow_count - 1)),
        ],
        compiler_params=pltpu.CompilerParams(
            collective_id=0, has_side_effects=True, vmem_limit_bytes=63 * 2**20
        ),
        name="transport",
    )(totals, courant, diffusion, *small)


def reciprocal(value):
    guess = pl.reciprocal(value, approx=True)
    guess = guess * (2.0 - value * guess)
    return guess * (2.0 - value * guess)


def solve_spd(entry, right):
    order = len(right)
    lower, scaled, inverse = {}, {}, []
    start = 0
    while start < order:
        size = min(2, order - start)
        block = range(start, start + size)
        work = {}
        for j in block:
            for i in range(j, order + 1):
                work[i, j] = right[j] if i == order else entry(i, j)
        for k in range(start):
            for i in range(start, order + 1):
                for j in block:
                    if i >= j:
                        work[i, j] = work[i, j] - lower[i, k] * scaled[j, k]
        for k in block:
            inverse.append(reciprocal(work[k, k]))
            for i in range(k + 1, order + 1):
                scaled[i, k] = work[i, k]
                lower[i, k] = work[i, k] * inverse[k]
            for j in range(k + 1, start + size):
                for i in range(j, order + 1):
                    work[i, j] = work[i, j] - lower[i, k] * scaled[j, k]
        start += size
        yield
    found = [lower[order, j] for j in range(order)]
    for i in reversed(range(order)):
        for j in range(i):
            found[j] = found[j] - lower[i, j] * found[i]
        if i % 4 == 0:
            yield
    return found


def together(*runs):
    runs = list(runs)
    while runs:
        runs = [run for run in runs if next(run, runs) is not runs]


def newton_kernel(
    secondary_count,
    totals_ref,
    exponent_lhs,
    pair_lhs,
    offset_ref,
    on_ref,
    front_ref,
    out_ref,
    *scratch,
):
    order, rows, width = totals_ref.shape
    group = rows // 2
    pairs = order * (order + 1) // 2
    place = {}
    for i in range(order):
        for j in range(i, order):
            place[j, i] = len(place)
    offset = offset_ref[...]
    offset = jnp.concatenate([offset, offset], axis=1)

    def total_of(base, i):
        return totals_ref[i, base : base + group, :]

    def sum_steps(base, y_ref, sums_ref):
        for s in range(0, group, 2):
            y = jnp.concatenate(
                [y_ref[pl.ds(s + h, order, stride=group), :] for h in range(2)], axis=1
            )
            y1, y2, y3 = parts(y, 3)
            exponent = jnp.dot(
                exponent_lhs[...],
                jnp.concatenate([y1, y2, y1, y3, y1, y2], axis=0),
                preferred_element_type=jnp.float32,
            )
            yield
            x = jnp.exp(exponent + offset)
            on = jnp.concatenate(
                [on_ref[base + s + h : base + s + h + 1, :] for h in range(2)], axis=1
            )
            x = jnp.concatenate([x[:secondary_count], x[secondary_count:] * on], axis=0)
            x1, x2 = parts(x, 2)
            sums = jnp.dot(
                pair_lhs[...],
                jnp.concatenate([x1, x2, x1, x2], axis=0),
                preferred_element_type=jnp.float32,
            )
            for h in range(2):
                sums_ref[pl.ds(s + h, pairs + order, stride=group), :] = sums[
                    : pairs + order, h * width : (h + 1) * width
                ]
            yield

    def update_steps(base, y_ref, sums_ref):
        def total(p):
            return sums_ref[p * group : (p + 1) * group, :]

        free = [jnp.exp(y_ref[i * group : (i + 1) * group, :]) for i in range(order)]
        residual = [free[i] + total(pairs + i) - total_of(base, i) for i in range(order)]

        def entry(i, j):
            value = total(place[i, j])
            return value + free[i] if i == j else value

        delta = yield from solve_spd(entry, residual)
        largest = [jnp.abs(v) for v in delta]
        while len(largest) > 1:
            largest = [jnp.maximum(a, b) for a, b in zip(largest[::2], largest[1::2])] + largest[
                len(largest) // 2 * 2 :
            ]
        scale = reciprocal(jnp.maximum(largest[0], 1.0))
        for i in range(order):
            part = slice(i * group, (i + 1) * group)
            y_ref[part, :] = y_ref[part, :] - delta[i] * scale

    early = (0, scratch[0], scratch[1])
    late = (group, scratch[2], scratch[3])
    for base, y_ref, _ in (early, late):
        for i in range(order):
            y_ref[i * group : (i + 1) * group, :] = jnp.log(total_of(base, i))
    together(sum_steps(*early))

    def iterate(_, carry):
        together(update_steps(*early), sum_steps(*late))
        together(update_steps(*late), sum_steps(*early))
        return carry

    lax.fori_loop(0, ITERS, iterate, 0)

    for base, y_ref, _ in (early, late):
        front = front_ref[base : base + group, :] > 0.0
        for i in range(order):
            out_ref[i, base : base + group, :] = jnp.where(
                front, y_ref[i * group : (i + 1) * group, :], jnp.log(total_of(base, i))
            )


def speciate(totals, exponent_lhs, pair_lhs, offset, on, front, secondary_count):
    order, rows, width = totals.shape
    group = 16
    sums = order * (order + 1) // 2 + order
    whole = pl.BlockSpec(memory_space=pltpu.VMEM)
    block = pl.BlockSpec((order, group, width), lambda i: (0, i, 0))
    per_row = pl.BlockSpec((group, width), lambda i: (i, 0))
    return pl.pallas_call(
        functools.partial(newton_kernel, secondary_count),
        grid=(rows // group,),
        out_shape=jax.ShapeDtypeStruct(totals.shape, jnp.float32),
        in_specs=[block, whole, whole, whole, per_row, per_row],
        out_specs=block,
        scratch_shapes=[
            pltpu.VMEM((order * group // 2, width), jnp.float32),
            pltpu.VMEM((sums * group // 2, width), jnp.float32),
        ]
        * 2,
        compiler_params=pltpu.CompilerParams(vmem_limit_bytes=63 * 2**20),
        name="newton",
    )(totals, exponent_lhs, pair_lhs, offset, on, front)


def shards(
    totals,
    courant,
    diffusion,
    stoich,
    log_k,
    mineral_stoich,
    mineral_log_k,
    mineral_rate,
    front_counts,
    mineral_flags,
):
    moved = transport(
        totals,
        courant,
        diffusion,
        stoich,
        log_k,
        mineral_stoich,
        mineral_log_k,
        mineral_rate,
        front_counts,
        mineral_flags,
    )
    return speciate(*moved, stoich.shape[0])


def solution(mesh):
    placed = (
        P("narrow", "wide", None),
        P("wide", None),
        P("wide", None),
        P(),
        P(),
        P(),
        P(),
        P(),
        P(),
        P("wide", "narrow"),
    )
    return jax.shard_map(
        shards, mesh=mesh, in_specs=placed, out_specs=P(None, "wide", "narrow"), check_vma=False
    )
```

```python
import functools

import jax
import jax.numpy as jnp
from jax import lax
from jax.experimental import pallas as pl
from jax.experimental.pallas import tpu as pltpu
from jax.sharding import PartitionSpec as P

STEPS = 4
ITERS = 4
MESH = pl.DeviceIdType.MESH


def parts(values, count):
    found = []
    for _ in range(count):
        part = values.astype(jnp.bfloat16)
        found.append(part)
        values = values - part.astype(jnp.float32)
    return found


def column_of(row):
    count = row.shape[1]
    shape = (count, count)
    same = lax.broadcasted_iota(jnp.int32, shape, 0) == lax.broadcasted_iota(jnp.int32, shape, 1)
    return jnp.sum(jnp.where(same, jnp.broadcast_to(row, shape), 0.0), axis=1, keepdims=True)


def build_tables(stoich, log_k, mineral_stoich, mineral_log_k, mineral_rate, refs):
    exponent_out, pair_out, offset_out, wide_f32, pair_f32 = refs
    order = stoich.shape[0]
    species, width = offset_out.shape
    split, used = stoich.shape[1], stoich.shape[1] + mineral_stoich.shape[0]
    offset_out[...] = jnp.zeros_like(offset_out)
    offset_out[0:split, :] = jnp.broadcast_to(column_of(log_k[...]), (split, width))
    offset_out[split:used, :] = jnp.broadcast_to(
        column_of(jnp.log(mineral_rate[...]) - mineral_log_k[...]), (used - split, width)
    )

    def copies(length, first, period, lanes):
        row = lax.broadcasted_iota(jnp.int32, (length, lanes), 0) + first
        lane = lax.broadcasted_iota(jnp.int32, (length, lanes), 1)
        return jnp.where(lane % period == row, 1.0, 0.0).astype(jnp.float32)

    def product(left, right, dim):
        return lax.dot_general(
            left,
            right,
            (((dim,), (0,)), ((), ())),
            precision=lax.Precision.HIGHEST,
            preferred_element_type=jnp.float32,
        )

    spread = copies(order, 0, order, 6 * order)
    wide_f32[...] = jnp.zeros_like(wide_f32)
    wide_f32[0:split, :] = product(stoich[...], spread, 0)
    wide_f32[split:used, :] = product(mineral_stoich[...], spread, 1)
    wide = wide_f32[...]
    first, second, third = parts(wide, 3)
    lane = lax.broadcasted_iota(jnp.int32, wide.shape, 1) // order
    exponent_out[...] = jnp.where(
        jnp.logical_or(lane == 2, lane == 5),
        second.astype(jnp.float32),
        jnp.where(lane == 4, third.astype(jnp.float32), first.astype(jnp.float32)),
    ).astype(jnp.bfloat16)
    tall = product(stoich[...], copies(split, 0, species, 4 * species), 1) + product(
        mineral_stoich[...], copies(used - split, split, species, 4 * species), 0
    )
    pair_f32[...] = jnp.zeros_like(pair_f32)
    start = 0
    for i in range(order):
        pair_f32[start : start + order - i, :] = tall[i:order, :] * tall[i : i + 1, :]
        start += order - i
    pair_f32[start : start + order, :] = tall
    first, second = parts(pair_f32[...], 2)
    lane = lax.broadcasted_iota(jnp.int32, pair_f32.shape, 1)
    pair_out[...] = jnp.where(
        lane < 2 * species, first.astype(jnp.float32), second.astype(jnp.float32)
    ).astype(jnp.bfloat16)


def transport_kernel(
    wide_count,
    narrow_count,
    totals_any,
    courant_any,
    diffusion_any,
    stoich_any,
    log_k_any,
    mineral_stoich_any,
    mineral_log_k_any,
    mineral_rate_any,
    counts_any,
    flags_any,
    out_ref,
    exponent_out,
    pair_out,
    offset_out,
    on_out,
    front_out,
    tall_f,
    tall_c,
    tall_d,
    stoich,
    log_k,
    mineral_stoich,
    mineral_log_k,
    mineral_rate,
    counts,
    flags,
    halo_out,
    halo_in,
    staged,
    wide_f32,
    pair_f32,
    local_sem,
    halo_send,
    halo_recv,
    swap_send,
    swap_recv,
):
    components, tall, columns = tall_f.shape
    rows, width = out_ref.shape[1:]
    pad = (tall - rows) // 2
    wide = lax.axis_index("wide")
    narrow = lax.axis_index("narrow")
    has_above = wide > 0
    has_below = wide < wide_count - 1
    peers = [lax.rem(narrow + d, narrow_count) for d in range(1, narrow_count)]
    inside = pl.ds(pad, rows)

    moves = [
        pltpu.make_async_copy(src, dst, local_sem.at[k])
        for k, (src, dst) in enumerate(
            (
                (totals_any, tall_f.at[:, inside, :]),
                (courant_any, tall_c.at[inside, :]),
                (diffusion_any, tall_d.at[inside, :]),
                (stoich_any, stoich),
                (log_k_any, log_k),
                (mineral_stoich_any, mineral_stoich),
                (mineral_log_k_any, mineral_log_k),
                (mineral_rate_any, mineral_rate),
                (counts_any, counts),
                (flags_any, flags),
            )
        )
    ]
    for move in moves:
        move.start()

    barrier = pltpu.get_barrier_semaphore()
    for peer in peers:
        pl.semaphore_signal(barrier, inc=1, device_id=(wide, peer), device_id_type=MESH)

    @pl.when(has_above)
    def _():
        pl.semaphore_signal(barrier, inc=1, device_id=(wide - 1, narrow), device_id_type=MESH)

    @pl.when(has_below)
    def _():
        pl.semaphore_signal(barrier, inc=1, device_id=(wide + 1, narrow), device_id_type=MESH)

    for ref in (tall_c, tall_d):
        for start in (0, pad + rows):
            ref[start : start + pad, :] = jnp.zeros((pad, columns), jnp.float32)
    for start in (0, pad + rows):
        tall_f[:, start : start + pad, :] = jnp.zeros((components, pad, columns), jnp.float32)

    for move in moves[:3]:
        move.wait()

    for side, start in ((0, pad + rows - STEPS), (1, pad)):
        for c in range(components):
            halo_out[side, c * STEPS : (c + 1) * STEPS, :] = tall_f[c, start : start + STEPS, :]
        end = components * STEPS
        halo_out[side, end : end + STEPS, :] = tall_c[start : start + STEPS, :]
        halo_out[side, end + STEPS : end + 2 * STEPS, :] = tall_d[start : start + STEPS, :]

    neighbours = narrow_count - 1 + has_above.astype(jnp.int32) + has_below.astype(jnp.int32)
    pl.semaphore_wait(barrier, neighbours)

    def halo_copy(side, target):
        return pltpu.make_async_remote_copy(
            src_ref=halo_out.at[side],
            dst_ref=halo_in.at[side],
            send_sem=halo_send.at[side],
            recv_sem=halo_recv.at[side],
            device_id=(target, narrow),
            device_id_type=MESH,
        )

    to_below = halo_copy(0, wide + 1)
    to_above = halo_copy(1, wide - 1)

    @pl.when(has_below)
    def _():
        to_below.start()

    @pl.when(has_above)
    def _():
        to_above.start()

    swaps = []

    def advance(phase, start, length, offset, kept):
        part = pl.ds(start, length)
        courant, diffusion = tall_c[part, :], tall_d[part, :]
        keep = 1.0 - courant - 4.0 * diffusion
        push = courant + diffusion
        column = lax.broadcasted_iota(jnp.int32, (length, width), 1)
        first, last = column == 0, column == width - 1
        target = pl.ds(start + offset - pad, kept)
        for c in range(components):
            fields = tall_f[c, part, :]
            for _ in range(STEPS):
                upwind = pltpu.roll(fields, 1, 0)
                downwind = pltpu.roll(fields, length - 1, 0)
                left = pltpu.roll(fields, 1, 1)
                left = jnp.concatenate(
                    [jnp.where(first, 0.0, left[:, :width]), left[:, width:]], axis=1
                )
                right = pltpu.roll(fields, columns - 1, 1)
                right = jnp.concatenate(
                    [right[:, :-width], jnp.where(last, 0.0, right[:, -width:])], axis=1
                )
                fields = keep * fields + push * upwind + diffusion * (downwind + (left + right))
            for p in range(narrow_count):
                staged[p, c, target, :] = fields[
                    offset : offset + kept, p * width : (p + 1) * width
                ]
            for k, peer in enumerate(peers):
                copy = pltpu.make_async_remote_copy(
                    src_ref=staged.at[peer, c, target, :],
                    dst_ref=out_ref.at[narrow * components + c, target, :],
                    send_sem=swap_send.at[phase, c, k],
                    recv_sem=swap_recv.at[phase, c, k],
                    device_id=(wide, peer),
                    device_id_type=MESH,
                )
                copy.start()
                swaps.append(copy)
            out_ref[narrow * components + c, target, :] = staged[narrow, c, target, :]

    advance(0, pad, rows, pad, rows - 2 * pad)
    def take(side, start):
        for c in range(components):
            tall_f[c, start : start + STEPS, :] = halo_in[side, c * STEPS : (c + 1) * STEPS, :]
        end = components * STEPS
        tall_c[start : start + STEPS, :] = halo_in[side, end : end + STEPS, :]
        tall_d[start : start + STEPS, :] = halo_in[side, end + STEPS : end + 2 * STEPS, :]

    @pl.when(has_above)
    def _():
        to_below.wait_recv()
        take(0, pad - STEPS)

    advance(1, 0, 3 * pad, pad, pad)

    @pl.when(has_below)
    def _():
        to_above.wait_recv()
        take(1, pad + rows)

    advance(2, rows - pad, 3 * pad, pad, pad)

    for move in moves[3:]:
        move.wait()
    build_tables(
        stoich,
        log_k,
        mineral_stoich,
        mineral_log_k,
        mineral_rate,
        (exponent_out, pair_out, offset_out, wide_f32, pair_f32),
    )
    blocks = flags.shape[1]
    row = lax.broadcasted_iota(jnp.int32, (rows, blocks), 0)
    mine = row // (rows // blocks) == lax.broadcasted_iota(jnp.int32, (rows, blocks), 1)
    flag_rows = jnp.broadcast_to(flags[...].astype(jnp.float32), (rows, blocks))
    on = jnp.sum(jnp.where(mine, flag_rows, 0.0), axis=1, keepdims=True)
    on_out[...] = jnp.broadcast_to(on, on_out.shape)
    row = lax.broadcasted_iota(jnp.int32, counts.shape, 0)
    lane = lax.broadcasted_iota(jnp.int32, counts.shape, 1)
    own = jnp.where(
        jnp.logical_and(row == narrow, lane == wide), counts[...].astype(jnp.float32), 0.0
    )
    own = jnp.sum(jnp.sum(own, axis=1, keepdims=True), axis=0, keepdims=True)
    row = lax.broadcasted_iota(jnp.int32, front_out.shape, 0) // (rows // blocks)
    front_out[...] = jnp.where(row.astype(jnp.float32) < own, 1.0, 0.0)

    @pl.when(has_below)
    def _():
        to_below.wait_send()

    @pl.when(has_above)
    def _():
        to_above.wait_send()

    for copy in swaps:
        copy.wait()


def transport(
    totals,
    courant,
    diffusion,
    stoich,
    log_k,
    mineral_stoich,
    mineral_log_k,
    mineral_rate,
    front_counts,
    mineral_flags,
):
    components, rows, columns = totals.shape
    wide_count, narrow_count = lax.axis_size("wide"), lax.axis_size("narrow")
    width = columns // narrow_count
    order = components * narrow_count
    tall = rows + 2 * 8
    packed = (components + 2) * STEPS
    species = -(-(stoich.shape[0] + mineral_stoich.shape[0]) // 16) * 16
    sums = order * (order + 1) // 2 + order
    sums_padded = -(-sums // 16) * 16
    vmem = pl.BlockSpec(memory_space=pltpu.VMEM)
    small = (
        stoich.T,
        log_k.reshape(1, -1),
        mineral_stoich,
        mineral_log_k.reshape(1, -1),
        mineral_rate.reshape(1, -1),
        front_counts.T,
        mineral_flags.reshape(1, -1),
    )
    f32 = jnp.float32
    outs = (
        ((order, rows, width), f32),
        ((species, 6 * order), jnp.bfloat16),
        ((sums_padded, 4 * species), jnp.bfloat16),
        ((species, width), f32),
        ((rows, width), f32),
        ((rows, width), f32),
    )
    return pl.pallas_call(
        functools.partial(transport_kernel, wide_count, narrow_count),
        out_shape=[jax.ShapeDtypeStruct(shape, dtype) for shape, dtype in outs],
        in_specs=[pl.BlockSpec(memory_space=pltpu.HBM)] * (3 + len(small)),
        out_specs=[vmem] * len(outs),
        scratch_shapes=[
            pltpu.VMEM((components, tall, columns), f32),
            pltpu.VMEM((tall, columns), f32),
            pltpu.VMEM((tall, columns), f32),
            *[pltpu.VMEM(array.shape, array.dtype) for array in small],
            pltpu.VMEM((2, packed, columns), f32),
            pltpu.VMEM((2, packed, columns), f32),
            pltpu.VMEM((narrow_count, components, rows, width), f32),
            pltpu.VMEM((species, 6 * order), f32),
            pltpu.VMEM((sums_padded, 4 * species), f32),
            pltpu.SemaphoreType.DMA((3 + len(small),)),
            pltpu.SemaphoreType.DMA((2,)),
            pltpu.SemaphoreType.DMA((2,)),
            pltpu.SemaphoreType.DMA((3, components, narrow_count - 1)),
            pltpu.SemaphoreType.DMA((3, components, narrow_count - 1)),
        ],
        compiler_params=pltpu.CompilerParams(
            collective_id=0, has_side_effects=True, vmem_limit_bytes=63 * 2**20
        ),
        name="transport",
    )(totals, courant, diffusion, *small)


def reciprocal(value):
    guess = pl.reciprocal(value, approx=True)
    return guess * (2.0 - value * guess)


def solve_spd(entry, right):
    order = len(right)
    lower, scaled, inverse = {}, {}, []
    start = 0
    while start < order:
        size = min(2, order - start)
        block = range(start, start + size)
        work = {}
        for j in block:
            for i in range(j, order + 1):
                work[i, j] = right[j] if i == order else entry(i, j)
        for k in range(start):
            for i in range(start, order + 1):
                for j in block:
                    if i >= j:
                        work[i, j] = work[i, j] - lower[i, k] * scaled[j, k]
        for k in block:
            inverse.append(reciprocal(work[k, k]))
            for i in range(k + 1, order + 1):
                scaled[i, k] = work[i, k]
                lower[i, k] = work[i, k] * inverse[k]
            for j in range(k + 1, start + size):
                for i in range(j, order + 1):
                    work[i, j] = work[i, j] - lower[i, k] * scaled[j, k]
        start += size
        yield
    found = [lower[order, j] for j in range(order)]
    for i in reversed(range(order)):
        for j in range(i):
            found[j] = found[j] - lower[i, j] * found[i]
        if i % 4 == 0:
            yield
    return found


def together(*runs):
    runs = list(runs)
    while runs:
        runs = [run for run in runs if next(run, runs) is not runs]


def newton_kernel(
    secondary_count,
    totals_ref,
    exponent_lhs,
    pair_lhs,
    offset_ref,
    on_ref,
    front_ref,
    out_ref,
    *scratch,
):
    order, rows, width = totals_ref.shape
    group = rows // 2
    pairs = order * (order + 1) // 2
    place = {}
    for i in range(order):
        for j in range(i, order):
            place[j, i] = len(place)
    offset = offset_ref[...]
    offset = jnp.concatenate([offset, offset], axis=1)

    def total_of(base, i):
        return totals_ref[i, base : base + group, :]

    def sum_steps(base, y_ref, sums_ref):
        for s in range(0, group, 2):
            y = jnp.concatenate(
                [y_ref[pl.ds(s + h, order, stride=group), :] for h in range(2)], axis=1
            )
            y1, y2, y3 = parts(y, 3)
            exponent = jnp.dot(
                exponent_lhs[...],
                jnp.concatenate([y1, y2, y1, y3, y1, y2], axis=0),
                preferred_element_type=jnp.float32,
            )
            yield
            x = jnp.exp(exponent + offset)
            on = jnp.concatenate(
                [on_ref[base + s + h : base + s + h + 1, :] for h in range(2)], axis=1
            )
            x = jnp.concatenate([x[:secondary_count], x[secondary_count:] * on], axis=0)
            x1, x2 = parts(x, 2)
            sums = jnp.dot(
                pair_lhs[...],
                jnp.concatenate([x1, x2, x1, x2], axis=0),
                preferred_element_type=jnp.float32,
            )
            for h in range(2):
                sums_ref[pl.ds(s + h, pairs + order, stride=group), :] = sums[
                    : pairs + order, h * width : (h + 1) * width
                ]
            yield

    def update_steps(base, y_ref, sums_ref):
        def total(p):
            return sums_ref[p * group : (p + 1) * group, :]

        free = [jnp.exp(y_ref[i * group : (i + 1) * group, :]) for i in range(order)]
        residual = [free[i] + total(pairs + i) - total_of(base, i) for i in range(order)]

        def entry(i, j):
            value = total(place[i, j])
            return value + free[i] if i == j else value

        delta = yield from solve_spd(entry, residual)
        largest = [jnp.abs(v) for v in delta]
        while len(largest) > 1:
            largest = [jnp.maximum(a, b) for a, b in zip(largest[::2], largest[1::2])] + largest[
                len(largest) // 2 * 2 :
            ]
        scale = reciprocal(jnp.maximum(largest[0], 1.0))
        for i in range(order):
            part = slice(i * group, (i + 1) * group)
            y_ref[part, :] = y_ref[part, :] - delta[i] * scale

    early = (0, scratch[0], scratch[1])
    late = (group, scratch[2], scratch[3])
    for base, y_ref, _ in (early, late):
        for i in range(order):
            y_ref[i * group : (i + 1) * group, :] = jnp.log(total_of(base, i))
    together(sum_steps(*early))

    def iterate(_, carry):
        together(update_steps(*early), sum_steps(*late))
        together(update_steps(*late), sum_steps(*early))
        return carry

    lax.fori_loop(0, ITERS, iterate, 0)

    for base, y_ref, _ in (early, late):
        front = front_ref[base : base + group, :] > 0.0
        for i in range(order):
            out_ref[i, base : base + group, :] = jnp.where(
                front, y_ref[i * group : (i + 1) * group, :], jnp.log(total_of(base, i))
            )


def speciate(totals, exponent_lhs, pair_lhs, offset, on, front, secondary_count):
    order, rows, width = totals.shape
    group = 16
    sums = order * (order + 1) // 2 + order
    whole = pl.BlockSpec(memory_space=pltpu.VMEM)
    block = pl.BlockSpec((order, group, width), lambda i: (0, i, 0))
    per_row = pl.BlockSpec((group, width), lambda i: (i, 0))
    return pl.pallas_call(
        functools.partial(newton_kernel, secondary_count),
        grid=(rows // group,),
        out_shape=jax.ShapeDtypeStruct(totals.shape, jnp.float32),
        in_specs=[block, whole, whole, whole, per_row, per_row],
        out_specs=block,
        scratch_shapes=[
            pltpu.VMEM((order * group // 2, width), jnp.float32),
            pltpu.VMEM((sums * group // 2, width), jnp.float32),
        ]
        * 2,
        compiler_params=pltpu.CompilerParams(vmem_limit_bytes=63 * 2**20),
        name="newton",
    )(totals, exponent_lhs, pair_lhs, offset, on, front)


def shards(
    totals,
    courant,
    diffusion,
    stoich,
    log_k,
    mineral_stoich,
    mineral_log_k,
    mineral_rate,
    front_counts,
    mineral_flags,
):
    moved = transport(
        totals,
        courant,
        diffusion,
        stoich,
        log_k,
        mineral_stoich,
        mineral_log_k,
        mineral_rate,
        front_counts,
        mineral_flags,
    )
    return speciate(*moved, stoich.shape[0])


def solution(mesh):
    placed = (
        P("narrow", "wide", None),
        P("wide", None),
        P("wide", None),
        P(),
        P(),
        P(),
        P(),
        P(),
        P(),
        P("wide", "narrow"),
    )
    return jax.shard_map(
        shards, mesh=mesh, in_specs=placed, out_specs=P(None, "wide", "narrow"), check_vma=False
    )
```
